256 devices in a mesh: pool: 32 (over x, y, core), tgt: 8 (over z).
Axes of the slice: x: 4, y: 4, z: 8, core: 2. Of those that a mesh axis runs over, the one named last changes fastest.
Arguments:
- pool_hidden: bfloat16 [32768, 14336], P('pool', 'tgt'), may hold values from -8 to 8
- pool_grad: bfloat16 [32768, 4096], P('pool', 'tgt'), may hold values from -8 to 8
- target_hidden: bfloat16 [49152, 14336], P('pool', 'tgt'), may hold values from -8 to 8
- target_grad: bfloat16 [49152, 4096], P('pool', 'tgt'), may hold values from -8 to 8
- in_factor: bfloat16 [14336, 128], P('tgt'), may hold values from -0.046875 to 0.046875
- out_factor: bfloat16 [4096, 64], P('tgt'), may hold values from -0.09375 to 0.09375
- example_of_token: int32 [256, 192], P(('pool', 'tgt')), may hold values from 0 to 15, never falling along the last dimension, each value on 1 to 24 neighbouring positions
- owner_map: int32 [32768, 1], P(('pool', 'tgt')), may hold values from 0 to 31; in each aligned block of 128 rows (0 to 127, 128 to 255, ...) at most 8 rows name the same one
Outputs:
- delivered_weight: float32 [32, 8, 32, 8], P('pool', 'tgt')
- delivered_token: int32 [32, 8, 32, 8], P('pool', 'tgt')
The draws below stay inside these ranges and needn't reach their ends.
Inputs may be any that keep to these rules, and one draw needn't show every extreme that they name: `example_of_token`: within each row, numbers never fall; every one of the 16 examples has 1 to 24 tokens, one exactly 24. `owner_map`: among the 128 tokens of one device at most 8 have the same owner; some owner gets exactly 8 from some device.
All inputs are finite; a program needn't handle non-finite values.
Results may differ from the reference program's by a relative error of at most 0.0028.
Values may be sent and summed in bfloat16 or wider, within the bound.
No kernel may reach another device: no remote copies, remote signals or barrier semaphores. Data moves between devices by JAX's collectives and lax.ppermute only.
A program may use at most 128 MiB of HBM per device.

```python
import math
import jax
import jax.numpy as jnp
import numpy as np
from jax import lax

D = 4096
FF = 14336
KH = 128
KG = 64
ROW_DEV = 128
TGT_SUB = 192
EX_DEV = 16
MOST_TOK = 24
CAP = 8
TOKENS_POOL = 32768
TGT_TOKENS = 49152
N_POOL = 32
N_TGT = 8


def shared_dirs(key):
    hidden_dirs = jax.random.normal(jax.random.fold_in(key, 901), (128, FF), jnp.float32)
    grad_dirs = jax.random.normal(jax.random.fold_in(key, 902), (128, D), jnp.float32)
    return (hidden_dirs, grad_dirs)


def pool_mixture(key, directions):
    picks = jax.random.randint(jax.random.fold_in(key, 903), (TOKENS_POOL, 3), 0, 128)
    shares = jax.random.uniform(jax.random.fold_in(key, 904), (TOKENS_POOL, 3), jnp.float32, 0.35, 0.75)
    mixed = shares[:, 0:1] * directions[picks[:, 0]]
    mixed = mixed + shares[:, 1:2] * directions[picks[:, 1]]
    mixed = mixed + shares[:, 2:3] * directions[picks[:, 2]]
    return mixed


def target_mixture(key, directions):
    run_picks = jax.random.randint(jax.random.fold_in(key, 905), ((TGT_TOKENS + 3) // 4,), 0, 128)
    rows = jnp.arange(TGT_TOKENS, dtype=jnp.int32) // 4
    return directions[run_picks[rows]]


def row_weights(key, rows, ramp_low, ramp_rise, spread):
    ramp = ramp_low + ramp_rise * jnp.arange(rows, dtype=jnp.float32) / rows
    return ramp * jnp.exp(jax.random.uniform(key, (rows,), jnp.float32, -spread, spread))


def draw_pool_hidden(key, part):
    hidden_dirs, grad_dirs = shared_dirs(key)
    mixed = pool_mixture(key, hidden_dirs)
    key = jax.random.fold_in(key, 11)
    keys = jax.random.split(key, 2)
    coef = row_weights(keys[0], TOKENS_POOL, 0.4, 1.2, 0.7)
    noise = jax.random.normal(keys[1], (TOKENS_POOL, FF), jnp.float32)
    return jnp.clip(coef[:, None] * mixed + noise, -8.0, 8.0).astype(jnp.bfloat16)


def draw_pool_grad(key, part):
    hidden_dirs, grad_dirs = shared_dirs(key)
    mixed = pool_mixture(key, grad_dirs)
    key = jax.random.fold_in(key, 12)
    keys = jax.random.split(key, 2)
    coef = row_weights(keys[0], TOKENS_POOL, 0.4, 1.2, 0.7)
    noise = jax.random.normal(keys[1], (TOKENS_POOL, D), jnp.float32)
    return jnp.clip(coef[:, None] * mixed + noise, -8.0, 8.0).astype(jnp.bfloat16)


def draw_target_hidden(key, part):
    hidden_dirs, grad_dirs = shared_dirs(key)
    mixed = target_mixture(key, hidden_dirs)
    key = jax.random.fold_in(key, 13)
    keys = jax.random.split(key, 2)
    coef = row_weights(keys[0], TGT_TOKENS, 0.8, 0.0, 1.0)
    noise = jax.random.normal(keys[1], (TGT_TOKENS, FF), jnp.float32)
    return jnp.clip(coef[:, None] * mixed + noise, -8.0, 8.0).astype(jnp.bfloat16)


def draw_target_grad(key, part):
    hidden_dirs, grad_dirs = shared_dirs(key)
    mixed = target_mixture(key, grad_dirs)
    key = jax.random.fold_in(key, 14)
    keys = jax.random.split(key, 2)
    coef = row_weights(keys[0], TGT_TOKENS, 0.8, 0.0, 1.0)
    noise = jax.random.normal(keys[1], (TGT_TOKENS, D), jnp.float32)
    return jnp.clip(coef[:, None] * mixed + noise, -8.0, 8.0).astype(jnp.bfloat16)


def level_of(stream_key, shape, pieces, low, high):
    loudness, own = 1.0, jax.random.fold_in(stream_key, 6)
    for position, parts in pieces:
        heights = jnp.exp(jax.random.uniform(jax.random.fold_in(own, position), (parts,), jnp.float32, low / len(pieces), high / len(pieces)))
        loudness = loudness * jnp.repeat(heights, shape[position] // parts).reshape([-1 if axis == position else 1 for axis in range(len(shape))])
    return loudness


def profile(count, total, reach, lean):
    loads = [(1 << 20) // math.isqrt(grade ** lean) + 1 for grade in range(2, count + 1)]
    spare, holding = total - reach - (count - 1), [1] * (count - 1)
    while spare > 0:
        movable = [i for i in range(count - 1) if holding[i] < reach]
        whole, remaining = sum([loads[i] for i in movable]), spare
        for i in movable:
            extra = min(reach - holding[i], max(1, remaining * loads[i] // whole), spare)
            holding[i] = holding[i] + extra
            spare = spare - extra
    return np.array([reach] + holding)


def ragged_sizes(stream_key, number_of, total, bound, lean):
    if number_of == 2:
        one = jax.random.randint(stream_key, (), max(1, total - bound), min(bound, total - 1) + 1)
        return jnp.stack([one, total - one])
    tallies = jnp.asarray(profile(number_of, total, bound, lean), jnp.int32)
    couples = (number_of - 1) // 2
    giver, sink = tallies[1:1 + 2 * couples:2], tallies[2:2 + 2 * couples:2]
    slack = jnp.minimum(giver - 1, bound - sink)
    passed = jax.random.randint(jax.random.fold_in(stream_key, 1), (couples,), 0, 1 << 20) % (slack + 1)
    tallies = tallies.at[1:1 + 2 * couples:2].set(giver - passed).at[2:2 + 2 * couples:2].set(sink + passed)
    return tallies[jax.random.permutation(jax.random.fold_in(stream_key, 2), number_of)]


def routed_block(rng, own, number, rows, count, top, limit, slope):
    order = jax.random.permutation(rng, count)
    heavy_load, usual = load_shares(count, rows * top, limit, slope, True), load_shares(count, rows * top, limit, slope, False)
    places = jnp.arange(count)

    def named(tallies, offset_by):
        used = int((tallies > 0).sum())
        fixed = max(1, used // 4)
        moved = fixed + (places - fixed + offset_by * (used - fixed)) % max(1, count - fixed)
        return jnp.zeros((count,), jnp.int32).at[order[jnp.where(places < fixed, places, moved)]].set(jnp.asarray(tallies, jnp.int32))

    tallies = jnp.where(number % 4 == 0, named(heavy_load, number // 4), named(usual, number - number // 4 - 1))
    mixed = jax.random.permutation(jax.random.fold_in(own, 3), count)
    source_of, receiver = mixed[0:count // 2 * 2:2], mixed[1:count // 2 * 2:2]
    room = jnp.minimum(tallies[source_of] - 1, limit - tallies[receiver]) // 2
    room = jnp.where((source_of == order[0]) | (receiver == order[0]) | (tallies[receiver] == 0), 0, jnp.maximum(room, 0))
    moved = jax.random.randint(jax.random.fold_in(own, 4), (count // 2,), 0, 1 << 20) % (room + 1)
    tallies = tallies.at[source_of].add(-moved).at[receiver].add(moved)
    items = jnp.searchsorted(jnp.cumsum(tallies), jnp.arange(rows * top), side="right").astype(jnp.int32)
    listing = items.reshape(top, rows).T
    listing = listing[jax.random.permutation(jax.random.fold_in(own, 1), rows)]
    offset_by = jax.random.randint(jax.random.fold_in(own, 2), (rows, 1), 0, top)
    return jnp.take_along_axis(listing, (jnp.arange(top)[None, :] + offset_by) % top, axis=1)


def load_shares(count, total, limit, slope, full):
    portions = [(1 << 20) // math.isqrt(standing ** slope) + 1 for standing in range(1, count + 1)]
    largest = limit if full else min(limit, max(-(-total // count), total * portions[0] // sum(portions)))
    least = 1 if total - largest >= count - 1 else 0
    given, rest = [largest] + [least] * (count - 1), total - largest - least * (count - 1)
    while rest > 0:
        free = [i for i in range(1, count) if given[i] < largest] or [i for i in range(1, count) if given[i] < limit]
        mass, left = sum([portions[i] for i in free]), rest
        for i in free:
            addition = min(limit - given[i], max(1, left * portions[i] // mass), rest)
            given[i] = given[i] + addition
            rest = rest - addition
    return np.array(given)


def normal_values(own_key, shape, width, limit, cuts=(), kind=jnp.bfloat16):
    factor_of = level_of(own_key, shape, cuts, -0.22, 0.18) if cuts else 1.0
    values = jax.random.normal(own_key, shape, jnp.float32) * width * factor_of
    return jnp.minimum(jnp.maximum(values, -limit), limit).astype(kind)


def setup_inputs(seed: int = 0) -> dict:
    streams_of = jax.random.split(jax.random.key(seed), 9)
    pool_hidden = draw_pool_hidden(jax.random.fold_in(streams_of[8], 71), 0)
    pool_grad = draw_pool_grad(jax.random.fold_in(streams_of[8], 71), 0)
    target_hidden = draw_target_hidden(jax.random.fold_in(streams_of[8], 71), 0)
    target_grad = draw_target_grad(jax.random.fold_in(streams_of[8], 71), 0)
    in_factor = normal_values(streams_of[4], (FF, KH), FF ** -0.5, 0.046875, ((0, 8),))
    out_factor = normal_values(streams_of[5], (D, KG), D ** -0.5, 0.09375, ((0, 8),))
    example_of_token = jax.vmap(lambda own: jnp.searchsorted(jnp.cumsum(ragged_sizes(own, EX_DEV, TGT_SUB, MOST_TOK, 2)), jnp.arange(TGT_SUB), side="right"))(jax.random.split(streams_of[6], (N_POOL * N_TGT))).reshape((N_POOL * N_TGT, TGT_SUB)).astype(jnp.int32)
    owner_map_keys = jax.random.split(jax.random.fold_in(streams_of[7], 1), TOKENS_POOL // ROW_DEV)
    owner_map_turns = jax.random.permutation(jax.random.fold_in(streams_of[7], 3), TOKENS_POOL // ROW_DEV)
    owner_map = jax.vmap(lambda own, number: routed_block(jax.random.fold_in(streams_of[7], 2), own, number, ROW_DEV, N_POOL, 1, CAP, 2))(owner_map_keys, owner_map_turns).reshape((TOKENS_POOL, 1))
    return dict(pool_hidden=pool_hidden, pool_grad=pool_grad, target_hidden=target_hidden, target_grad=target_grad, in_factor=in_factor, out_factor=out_factor, example_of_token=example_of_token, owner_map=owner_map)


def reference(pool_hidden, pool_grad, target_hidden, target_grad, in_factor, out_factor, example_of_token, owner_map):
    highest = lax.Precision.HIGHEST
    blocks = N_POOL * N_TGT
    rows_block = ROW_DEV * N_TGT
    pool_in = jnp.dot(pool_hidden, in_factor, preferred_element_type=jnp.float32)
    pool_out = jnp.dot(pool_grad, out_factor, preferred_element_type=jnp.float32)
    pool_scale = lax.rsqrt(lax.optimization_barrier(jnp.sum(pool_in * pool_in, axis=1)) * lax.optimization_barrier(jnp.sum(pool_out * pool_out, axis=1)) + 1e-06)
    target_in = jnp.dot(target_hidden, in_factor, preferred_element_type=jnp.float32).reshape(blocks, TGT_SUB, KH)
    target_out = jnp.dot(target_grad, out_factor, preferred_element_type=jnp.float32).reshape(blocks, TGT_SUB, KG)
    example_hot = (example_of_token[:, :, None] == jnp.arange(EX_DEV, dtype=jnp.int32)[None, None, :]).astype(jnp.float32)
    gram_in = jnp.einsum('bsk,brk->bsr', target_in, target_in, precision=highest)
    gram_out = jnp.einsum('bsk,brk->bsr', target_out, target_out, precision=highest)
    spread = jnp.einsum('bsr,bre->bse', gram_in * gram_out, example_hot, precision=highest)
    norm_sq = lax.optimization_barrier(jnp.sum(example_hot * spread, axis=1))
    token_sq = lax.optimization_barrier(jnp.sum(example_hot * norm_sq[:, None, :], axis=2))
    token_scale = lax.rsqrt(token_sq + 1e-06)
    scaled_in = (target_in * token_scale[:, :, None]).astype(jnp.bfloat16).reshape(-1, KH)
    target_low = target_out.astype(jnp.bfloat16).reshape(-1, KG)
    left_in = pool_in.astype(jnp.bfloat16).reshape(-1, rows_block, KH)
    left_out = pool_out.astype(jnp.bfloat16).reshape(-1, rows_block, KG)

    def score_block(operands):
        block_in, block_out = operands
        match_in = jnp.dot(block_in, scaled_in.T, preferred_element_type=jnp.float32)
        match_out = jnp.dot(block_out, target_low.T, preferred_element_type=jnp.float32)
        joined = lax.optimization_barrier((match_in * match_out).astype(jnp.bfloat16))
        joined = joined.astype(jnp.float32).reshape(rows_block, blocks, TGT_SUB)
        per_example = jnp.einsum('rbs,bse->rbe', joined, example_hot, precision=highest)
        return lax.optimization_barrier(jnp.max(per_example, axis=(1, 2)))
    best_match = lax.map(score_block, (left_in, left_out)).reshape(-1)
    score = best_match * pool_scale
    weight = score * lax.rsqrt(jnp.sum(score * score) / TOKENS_POOL + 1e-06)
    weights_blocked = weight.reshape(blocks, ROW_DEV)
    owners = owner_map.reshape(blocks, ROW_DEV)
    owner_hot = (owners[:, :, None] == jnp.arange(N_POOL, dtype=jnp.int32)[None, None, :]).astype(jnp.int32)
    ranking = lax.optimization_barrier(jnp.sum(jnp.cumsum(owner_hot, axis=1) * owner_hot, axis=2)) - 1
    select = (owner_hot[:, :, :, None] > 0) & (ranking[:, :, None, None] == jnp.arange(CAP, dtype=jnp.int32)[None, None, None, :])
    slot_weight = lax.optimization_barrier(jnp.sum(jnp.where(select, weights_blocked[:, :, None, None], jnp.float32(0.0)), axis=1))
    token_ids = jnp.arange(TOKENS_POOL, dtype=jnp.int32).reshape(blocks, ROW_DEV)
    slot_token = lax.optimization_barrier(jnp.sum(jnp.where(select, token_ids[:, :, None, None], 0), axis=1))
    slot_token = jnp.where(jnp.any(select, axis=1), slot_token, -1).astype(jnp.int32)
    slot_weight = jnp.transpose(slot_weight.reshape(N_POOL, N_TGT, N_POOL, CAP), (2, 1, 0, 3))
    slot_token = jnp.transpose(slot_token.reshape(N_POOL, N_TGT, N_POOL, CAP), (2, 1, 0, 3))
    return (slot_weight, slot_token)
```

```python
import functools

import jax
import jax.numpy as jnp
from jax import lax
from jax.experimental import pallas as pl
from jax.experimental.pallas import tpu as pltpu
from jax.sharding import PartitionSpec as P

KH = 128
KG = 64
ROWS = 128
TOK = 192
EX = 16
CAP = 8
GROUP = 8
F32 = jnp.float32
BF16 = jnp.bfloat16
HIGHEST = lax.Precision.HIGHEST
MSG = ROWS + TOK + (ROWS + TOK) // 2
TMSG = TOK + TOK // 2 + 16
PMSG = ROWS + ROWS // 2
MB = 1024 * 1024


def dot_nt(a, b, precision=None):
    return lax.dot_general(
        a, b, (((1,), (1,)), ((), ())), preferred_element_type=F32, precision=precision
    )


def lane_mask(shape, low):
    lane = lax.broadcasted_iota(jnp.int32, shape, 1)
    return (lane < KG) if low else (lane >= KG)


def project_kernel(order, s_ref, ph, pg, th, tg, fin, fout, *rest):
    outs, lo_ref, hi_ref = rest[:-2], rest[-2], rest[-1]
    step = pl.program_id(0)

    @pl.when(step == 0)
    def _():
        zero = jnp.zeros(fout.shape, BF16)
        lo_ref[...] = jnp.concatenate([fout[...], zero], axis=1)
        hi_ref[...] = jnp.concatenate([zero, fout[...]], axis=1)

    dot = functools.partial(jnp.dot, preferred_element_type=F32)
    pool_in = dot(ph[...], fin[...])
    tgt_in = dot(th[...], fin[...])
    half = ROWS // 2
    pool_out = dot(pg[0:half, :], lo_ref[...]) + dot(pg[half:ROWS, :], hi_ref[...])
    half = TOK // 2
    tgt_out = dot(tg[0:half, :], lo_ref[...]) + dot(tg[half:TOK, :], hi_ref[...])
    for i, out in enumerate(outs):

        @pl.when(step == i)
        def _(out=out):
            out[0:ROWS, :] = pool_in.astype(out.dtype)
            out[ROWS : ROWS + TOK, :] = tgt_in.astype(out.dtype)
            out[ROWS + TOK : ROWS + TOK + ROWS // 2, :] = pool_out.astype(out.dtype)
            out[ROWS + TOK + ROWS // 2 : MSG, :] = tgt_out.astype(out.dtype)


def project(t, order, ph, pg, th, tg, fin, fout):
    n = 8
    table = (t + jnp.array(order, jnp.int32)) % n
    row = lambda i, s: (s[i], 0)
    fixed = lambda i, s: (0, 0)
    return pl.pallas_call(
        functools.partial(project_kernel, order),
        grid_spec=pltpu.PrefetchScalarGridSpec(
            num_scalar_prefetch=1,
            grid=(len(order),),
            in_specs=[
                pl.BlockSpec((ROWS, ph.shape[1]), row),
                pl.BlockSpec((ROWS, pg.shape[1]), row),
                pl.BlockSpec((TOK, th.shape[1]), row),
                pl.BlockSpec((TOK, tg.shape[1]), row),
                pl.BlockSpec(fin.shape, fixed),
                pl.BlockSpec(fout.shape, fixed),
            ],
            out_specs=[pl.BlockSpec((MSG, KH), fixed) for _ in order],
            scratch_shapes=[pltpu.VMEM((fout.shape[0], 2 * KG), BF16)] * 2,
        ),
        out_shape=[jax.ShapeDtypeStruct((MSG, KH), BF16 if k else F32) for k in order],
        compiler_params=pltpu.CompilerParams(vmem_limit_bytes=24 * MB),
        cost_estimate=pl.CostEstimate(
            flops=len(order) * 170_000_000, bytes_accessed=len(order) * 1_600_000, transcendentals=0
        ),
        name="project",
    )(table, ph, pg, th, tg, fin, fout)


def prepare_kernel(own, *rest):
    parts, ids_ref, tmsg, pmsg, scale_ref = rest[:7], rest[7], rest[8], rest[9], rest[10]
    total = own[...]
    for part in parts:
        total = total + part[...].astype(F32)
    pool_in = total[0:ROWS]
    tgt_in = total[ROWS : ROWS + TOK]
    pool_out = total[ROWS + TOK : ROWS + TOK + ROWS // 2]
    tgt_out = total[ROWS + TOK + ROWS // 2 : MSG]

    pmsg[0:ROWS, :] = pool_in.astype(BF16)
    pmsg[ROWS:PMSG, :] = pool_out.astype(BF16)
    low = lane_mask(pool_out.shape, True)
    zero = jnp.zeros_like(pool_out)
    out_rows = jnp.concatenate(
        [jnp.where(low, pool_out, zero), jnp.where(low, zero, pool_out)], axis=0
    )
    in_sq = jnp.sum((pool_in * pool_in).T, axis=0, keepdims=True)
    out_sq = jnp.sum((out_rows * out_rows).T, axis=0, keepdims=True)
    scale_ref[...] = jnp.broadcast_to(lax.rsqrt(in_sq * out_sq + 1e-06), scale_ref.shape)

    ids = ids_ref[...].astype(F32)
    first = ids[0:1, :]
    second = jnp.where(lane_mask((1, KH), True), ids[1:2, :], -1.0)
    column = jnp.concatenate(
        [jnp.broadcast_to(first, (KH, KH)).T, jnp.broadcast_to(second, (KH, KH)).T], axis=0
    )
    same = jnp.concatenate([column == first, column == second], axis=1)
    pad = jnp.zeros((2 * KH - TOK, KH), F32)
    wide_in = jnp.concatenate([tgt_in, pad], axis=0)
    low = lane_mask(tgt_out.shape, True)
    zero = jnp.zeros_like(tgt_out)
    wide_out = jnp.concatenate(
        [
            jnp.where(low, tgt_out, zero),
            jnp.where(low, pltpu.roll(tgt_out, KG, 1), zero),
            pad,
        ],
        axis=0,
    )
    gram = dot_nt(wide_in, wide_in, HIGHEST) * dot_nt(wide_out, wide_out, HIGHEST)
    spread = jnp.sum(jnp.where(same, gram, 0.0), axis=0, keepdims=True)
    token_sq = jnp.sum(jnp.where(same, spread, 0.0), axis=1, keepdims=True)
    scaled = (tgt_in * lax.rsqrt(token_sq[0:TOK] + 1e-06)).astype(BF16)
    low_out = tgt_out.astype(BF16)
    ids_low = ids_ref[...]
    for i in range(tmsg.shape[0]):
        tmsg[i, 0:TOK, :] = scaled
        tmsg[i, TOK : TOK + TOK // 2, :] = low_out
        tmsg[i, TOK + TOK // 2 : TMSG, :] = ids_low


def prepare(own, parts, ids, copies):
    return pl.pallas_call(
        prepare_kernel,
        out_shape=[
            jax.ShapeDtypeStruct((copies, TMSG, KH), BF16),
            jax.ShapeDtypeStruct((PMSG, KH), BF16),
            jax.ShapeDtypeStruct((8, ROWS), F32),
        ],
        compiler_params=pltpu.CompilerParams(vmem_limit_bytes=24 * MB),
        cost_estimate=pl.CostEstimate(flops=200_000_000, bytes_accessed=3_000_000, transcendentals=0),
        name="prepare",
    )(own, *parts, ids)


def score_kernel(last, t_ref, *refs):
    pools, refs = refs[:8], refs[8:]
    if last:
        tmsg, prev, scale, out, pin, pout, t_in, t_out, hot, best, rows = refs
    else:
        tmsg, out, pin, pout, t_in, t_out, hot, best, rows = refs
    half = ROWS // 2
    low = lane_mask((half, KH), True)
    for k, pool in enumerate(pools):
        pin[k * ROWS : (k + 1) * ROWS, :] = pool[0:ROWS, :]
        packed = pool[ROWS:PMSG, :].astype(F32)
        turned = pltpu.roll(packed, KG, 1)
        pout[k * ROWS : k * ROWS + half, :] = jnp.where(low, packed, turned).astype(BF16)
        pout[k * ROWS + half : (k + 1) * ROWS, :] = jnp.where(low, turned, packed).astype(BF16)
    best[...] = jnp.full(best.shape, -jnp.inf, F32)

    lane = lax.broadcasted_iota(jnp.int32, (1, KH), 1)
    keep_low = (lane < KG).astype(F32).astype(BF16)
    keep_high = (lane >= KG).astype(F32).astype(BF16)
    width = GROUP * TOK
    tile = 256
    example = lax.broadcasted_iota(jnp.int32, (GROUP * EX, KH), 0).astype(F32)

    def group(g, carry):
        for pair in range(GROUP // 2):
            b0 = g * GROUP + 2 * pair
            b1 = b0 + 1
            at = pair * 2 * TOK
            t_in[at : at + TOK, :] = tmsg[b0, 0:TOK, :]
            t_in[at + TOK : at + TOK + 64, :] = tmsg[b1, 128:TOK, :]
            t_in[at + TOK + 64 : at + 2 * TOK, :] = tmsg[b1, 0:128, :]
            o0 = tmsg[b0, TOK : TOK + 96, :]
            o1 = tmsg[b1, TOK : TOK + 96, :]
            t_out[at : at + 96, :] = o0 * keep_low
            t_out[at + 96 : at + TOK, :] = o0 * keep_high
            t_out[at + TOK : at + TOK + 64, :] = o1[32:96] * keep_high
            t_out[at + TOK + 64 : at + TOK + 160, :] = o1 * keep_low
            t_out[at + TOK + 160 : at + 2 * TOK, :] = o1[0:32] * keep_high
            i0 = tmsg[b0, TOK + 96 : TMSG, :].astype(F32) + float(2 * pair * EX)
            i1 = tmsg[b1, TOK + 96 : TMSG, :].astype(F32) + float((2 * pair + 1) * EX)
            mixed = jnp.where(lane < KG, i0[1:2, :], i1[1:2, :])
            hot[:, at : at + 128] = (example == i0[0:1, :]).astype(F32).astype(BF16)
            hot[:, at + 128 : at + 256] = (example == mixed).astype(F32).astype(BF16)
            hot[:, at + 256 : at + 384] = (example == i1[0:1, :]).astype(F32).astype(BF16)

        chunk = 256

        def rows_of(c, carry):
            at = pl.ds(pl.multiple_of(c * chunk, chunk), chunk)
            left_in = pin[at, :]
            left_out = pout[at, :]
            total = None
            for i in range(width // tile):
                cols = slice(i * tile, (i + 1) * tile)
                joined = dot_nt(left_in, t_in[cols, :]) * dot_nt(left_out, t_out[cols, :])
                part = dot_nt(joined.astype(BF16), hot[:, cols])
                total = part if total is None else total + part
            best[at, :] = jnp.maximum(best[at, :], total)
            return carry

        return lax.fori_loop(0, pin.shape[0] // chunk, rows_of, carry)

    lax.fori_loop(0, tmsg.shape[0] // GROUP, group, 0)
    t = t_ref[0]
    for k in range(8):
        row = jnp.max(best[k * ROWS : (k + 1) * ROWS, :].T, axis=0, keepdims=True)
        rows[pl.ds(lax.rem(t + 8 - k, 8), 1), :] = row
    if last:
        final = jnp.maximum(rows[...], prev[...])
        for i in range(out.shape[0]):
            out[i, 0:8, :] = final
            out[i, 8:16, :] = scale[...]
    else:
        out[...] = rows[...]


def score(t, pools, tmsg, *more):
    last = len(more) > 0
    width = GROUP * TOK
    shape = (8, 16, ROWS) if last else (8, ROWS)
    vmem = pl.BlockSpec(memory_space=pltpu.VMEM)
    return pl.pallas_call(
        functools.partial(score_kernel, last),
        in_specs=[pl.BlockSpec(memory_space=pltpu.SMEM)] + [vmem] * (9 + len(more)),
        out_specs=vmem,
        out_shape=jax.ShapeDtypeStruct(shape, F32),
        scratch_shapes=[
            pltpu.VMEM((8 * ROWS, KH), BF16),
            pltpu.VMEM((8 * ROWS, KH), BF16),
            pltpu.VMEM((width, KH), BF16),
            pltpu.VMEM((width, KH), BF16),
            pltpu.VMEM((GROUP * EX, width), BF16),
            pltpu.VMEM((8 * ROWS, GROUP * EX), F32),
            pltpu.VMEM((8, ROWS), F32),
        ],
        compiler_params=pltpu.CompilerParams(vmem_limit_bytes=24 * MB),
        cost_estimate=pl.CostEstimate(
            flops=5_000_000_000, bytes_accessed=2_000_000, transcendentals=0
        ),
        name="score_last" if last else "score_first",
    )(t[None], *pools, tmsg, *more)


def slots_kernel(t_ref, got, owner, out):
    t = t_ref[0]
    first = t_ref[1]
    best = got[0, 0:8, :]
    for i in range(1, 8):
        best = jnp.maximum(best, got[i, 0:8, :])
    sub = lax.broadcasted_iota(jnp.int32, (8, ROWS), 0)
    scale = jnp.zeros((8, ROWS), F32)
    for i in range(8):
        scale = jnp.where(sub == i, got[i, 8:16, :], scale)
    value = best * scale
    square = jnp.sum(value * value)
    mine = jnp.sum(jnp.where(sub == t, value, 0.0), axis=0, keepdims=True)

    column = jnp.broadcast_to(owner[...].astype(F32), (ROWS, ROWS))
    across = column.T
    row = lax.broadcasted_iota(jnp.int32, (ROWS, ROWS), 0)
    lane = lax.broadcasted_iota(jnp.int32, (ROWS, ROWS), 1)
    earlier = jnp.where((column == across) & (row < lane), 1.0, 0.0)
    rank = jnp.sum(earlier, axis=0, keepdims=True)
    number = (first + 1 + lax.broadcasted_iota(jnp.int32, (1, ROWS), 1)).astype(F32)
    owned = jnp.where(across[0:32] == row[0:32].astype(F32), 1.0, 0.0)
    slot = row.astype(F32)
    filled = jnp.where(slot == rank, mine, 0.0) + jnp.where(slot == rank + CAP, number, 0.0)
    placed = dot_nt(owned, jnp.where(row < 2 * CAP, filled, 0.0), HIGHEST)
    out[...] = jnp.where(lane[0:32] == 2 * CAP, square, placed)


def slots(t, first, got, owner):
    vmem = pl.BlockSpec(memory_space=pltpu.VMEM)
    return pl.pallas_call(
        slots_kernel,
        in_specs=[pl.BlockSpec(memory_space=pltpu.SMEM), vmem, vmem],
        out_specs=vmem,
        out_shape=jax.ShapeDtypeStruct((32, ROWS), F32),
        name="slots",
    )(jnp.stack([t, first]), got, owner)


def finish_kernel(tokens, got, weight, token):
    square = jnp.sum(got[:, 2 * CAP : 2 * CAP + 1])
    norm = lax.rsqrt(jnp.full((1, CAP), square / tokens + 1e-06, F32))
    weight[...] = got[:, 0:CAP] * norm
    token[...] = got[:, CAP : 2 * CAP].astype(jnp.int32) - 1


def finish(got, tokens):
    return pl.pallas_call(
        functools.partial(finish_kernel, tokens),
        out_shape=[
            jax.ShapeDtypeStruct((32, CAP), F32),
            jax.ShapeDtypeStruct((32, CAP), jnp.int32),
        ],
        name="finish",
    )(got)


def shift(x, axis, n, k):
    return lax.ppermute(x, axis, [(i, (i + k) % n) for i in range(n)])


def shards(ph, pg, th, tg, fin, fout, example, owner):
    n_tgt = lax.axis_size("tgt")
    n_pool = lax.axis_size("pool")
    t = lax.axis_index("tgt")
    p = lax.axis_index("pool")
    ids = jnp.zeros((16, KH), BF16)
    wide = example.astype(BF16)
    ids = ids.at[0:1, :].set(wide[:, 0:KH])
    ids = ids.at[1:2, :].set(jnp.concatenate([wide[:, KH:TOK]] * 2, axis=1))

    order = (4, 3, 5, 2, 6, 1, 7, 0)
    messages = project(t, order, ph, pg, th, tg, fin, fout)
    parts = [shift(messages[i], "tgt", n_tgt, k) for i, k in enumerate(order) if k]
    tmsg, pmsg, scale = prepare(messages[-1], parts, ids, n_pool // 2)

    same_core = [[2 * i + c for i in range(n_pool // 2)] for c in range(2)]
    near = lax.all_to_all(
        tmsg, "pool", split_axis=0, concat_axis=0, tiled=True, axis_index_groups=same_core
    )
    pools = [pmsg] + [shift(pmsg, "tgt", n_tgt, k) for k in range(1, n_tgt)]
    far = lax.ppermute(near, "pool", [(i, i ^ 1) for i in range(n_pool)])
    partial = score(t, pools, near)
    best = score(t, pools, far, partial, scale)
    got = lax.all_to_all(best, "tgt", split_axis=0, concat_axis=0, tiled=True)
    sent = slots(t, (p * n_tgt + t) * ROWS, got, owner)
    arrived = lax.all_to_all(sent, "pool", split_axis=0, concat_axis=0, tiled=True)
    weight, token = finish(arrived, float(n_pool * n_tgt * ROWS))
    return (weight[None, None], token[None, None])


def solution(mesh):
    rows = P("pool", "tgt")
    both = P(("pool", "tgt"), None)
    placed = (rows, rows, rows, rows, P("tgt", None), P("tgt", None), both, both)
    return jax.shard_map(
        shards,
        mesh=mesh,
        in_specs=placed,
        out_specs=(P("pool", "tgt", None, None), P("pool", "tgt", None, None)),
        check_vma=False,
    )
```

```python
import functools

import jax
import jax.numpy as jnp
from jax import lax
from jax.experimental import pallas as pl
from jax.experimental.pallas import tpu as pltpu
from jax.sharding import PartitionSpec as P

KH = 128
KG = 64
ROWS = 128
TOK = 192
EX = 16
CAP = 8
GROUP = 8
F32 = jnp.float32
BF16 = jnp.bfloat16
HIGHEST = lax.Precision.HIGHEST
MSG = ROWS + TOK + (ROWS + TOK) // 2
TMSG = TOK + TOK // 2 + 16
PMSG = ROWS + ROWS // 2
MB = 1024 * 1024
LIMITS = (53, 53, 53)


def dot_nt(a, b, precision=None):
    return lax.dot_general(
        a, b, (((1,), (1,)), ((), ())), preferred_element_type=F32, precision=precision
    )


def lane_mask(shape, low):
    lane = lax.broadcasted_iota(jnp.int32, shape, 1)
    return (lane < KG) if low else (lane >= KG)


def project_kernel(steps, kinds, t_ref, ph, pg, th, tg, fin, fout, *rest):
    outs, (rows_in, rows_out, fin_v, fout_v, sems) = rest[:-5], rest[-5:]
    t = t_ref[0]
    weights = [
        pltpu.make_async_copy(fout, fout_v, sems.at[0, 0]),
        pltpu.make_async_copy(fin, fin_v, sems.at[0, 1]),
    ]
    for copy in weights:
        copy.start()
    moves = []
    both = ROWS + TOK
    for i, k in enumerate(steps):
        who = lax.rem(t + k, 8)
        pool = pl.ds(pl.multiple_of(who * ROWS, ROWS), ROWS)
        tgt = pl.ds(pl.multiple_of(who * TOK, TOK), TOK)
        at_pool = pl.ds(i * both, ROWS)
        at_tgt = pl.ds(i * both + ROWS, TOK)
        here = [
            pltpu.make_async_copy(pg.at[pool, :], rows_out.at[at_pool, :], sems.at[i + 1, 0]),
            pltpu.make_async_copy(tg.at[tgt, :], rows_out.at[at_tgt, :], sems.at[i + 1, 1]),
            pltpu.make_async_copy(ph.at[pool, :], rows_in.at[at_pool, :], sems.at[i + 1, 2]),
            pltpu.make_async_copy(th.at[tgt, :], rows_in.at[at_tgt, :], sems.at[i + 1, 3]),
        ]
        for copy in here:
            copy.start()
        moves.append(here)
    for copy in weights:
        copy.wait()
    together = min(2, len(steps))
    for first in range(0, len(steps), together):
        count = min(together, len(steps) - first)
        for i in range(first, first + count):
            for copy in moves[i]:
                copy.wait()
        rows = slice(first * both, (first + count) * both)
        sums_out = dot_nt(rows_out[rows, :], fout_v[...])
        sums_in = jnp.dot(rows_in[rows, :], fin_v[...], preferred_element_type=F32)
        for i in range(first, first + count):
            which, slot = kinds[i]
            out = outs[which]
            lead = (i - first) * both
            at = slot * MSG
            out[at : at + both, :] = sums_in[lead : lead + both].astype(out.dtype)
            at = at + both
            for size in (ROWS, TOK):
                half = size // 2
                packed = jnp.concatenate(
                    [sums_out[lead : lead + half], sums_out[lead + half : lead + size]], axis=1
                )
                out[at : at + half, :] = packed.astype(out.dtype)
                lead = lead + size
                at = at + half


def project(limit, t, steps, kinds, dtypes, ph, pg, th, tg, fin, fout):
    n = len(steps)
    sizes = [sum(1 for which, _ in kinds if which == j) for j in range(len(dtypes))]
    hbm = pl.BlockSpec(memory_space=pltpu.HBM)
    vmem = pl.BlockSpec(memory_space=pltpu.VMEM)
    return pl.pallas_call(
        functools.partial(project_kernel, steps, kinds),
        in_specs=[pl.BlockSpec(memory_space=pltpu.SMEM)] + [hbm] * 6,
        out_specs=[vmem for _ in dtypes],
        out_shape=[jax.ShapeDtypeStruct((c * MSG, KH), d) for c, d in zip(sizes, dtypes)],
        scratch_shapes=[
            pltpu.VMEM((n * (ROWS + TOK), ph.shape[1]), BF16),
            pltpu.VMEM((n * (ROWS + TOK), pg.shape[1]), BF16),
            pltpu.VMEM(fin.shape, BF16),
            pltpu.VMEM(fout.shape, BF16),
            pltpu.SemaphoreType.DMA((n + 1, 4)),
        ],
        compiler_params=pltpu.CompilerParams(vmem_limit_bytes=limit * MB),
        cost_estimate=pl.CostEstimate(
            flops=n * 170_000_000, bytes_accessed=n * 1_600_000, transcendentals=0
        ),
        name="project",
    )(t[None], ph, pg, th, tg, fin, fout)


def merge_kernel(from_low, from_high, mine_up, mine_down, up, down):
    up[...] = (mine_up[...] + from_low[MSG : 2 * MSG, :].astype(F32)).astype(BF16)
    down[...] = (mine_down[...] + from_high[MSG : 2 * MSG, :].astype(F32)).astype(BF16)


def merge(*operands):
    return pl.pallas_call(
        merge_kernel,
        out_shape=[jax.ShapeDtypeStruct((MSG, KH), BF16)] * 2,
        compiler_params=pltpu.CompilerParams(vmem_limit_bytes=8 * MB),
        cost_estimate=pl.CostEstimate(flops=200_000, bytes_accessed=1_500_000, transcendentals=0),
        name="merge",
    )(*operands)


def prepare_kernel(own, *rest):
    parts, (ids_ref, tmsg, pmsg, scale_ref) = rest[:-4], rest[-4:]
    total = own[...]
    for part in parts:
        total = total + part[0:MSG, :].astype(F32)
    pool_in = total[0:ROWS]
    tgt_in = total[ROWS : ROWS + TOK]
    pool_out = total[ROWS + TOK : ROWS + TOK + ROWS // 2]
    tgt_out = total[ROWS + TOK + ROWS // 2 : MSG]

    pmsg[0:ROWS, :] = pool_in.astype(BF16)
    pmsg[ROWS:PMSG, :] = pool_out.astype(BF16)
    low = lane_mask(pool_out.shape, True)
    zero = jnp.zeros_like(pool_out)
    out_rows = jnp.concatenate(
        [jnp.where(low, pool_out, zero), jnp.where(low, zero, pool_out)], axis=0
    )
    in_sq = jnp.sum((pool_in * pool_in).T, axis=0, keepdims=True)
    out_sq = jnp.sum((out_rows * out_rows).T, axis=0, keepdims=True)
    scale_ref[...] = jnp.broadcast_to(lax.rsqrt(in_sq * out_sq + 1e-06), scale_ref.shape)

    ids = ids_ref[...].astype(F32)
    first = ids[0:1, :]
    second = jnp.where(lane_mask((1, KH), True), ids[1:2, :], -1.0)
    column = jnp.concatenate(
        [jnp.broadcast_to(first, (KH, KH)).T, jnp.broadcast_to(second, (KH, KH)).T], axis=0
    )
    same = jnp.concatenate([column == first, column == second], axis=1)
    pad = jnp.zeros((2 * KH - TOK, KH), F32)
    wide_in = jnp.concatenate([tgt_in, pad], axis=0)
    low = lane_mask(tgt_out.shape, True)
    zero = jnp.zeros_like(tgt_out)
    wide_out = jnp.concatenate(
        [
            jnp.where(low, tgt_out, zero),
            jnp.where(low, pltpu.roll(tgt_out, KG, 1), zero),
            pad,
        ],
        axis=0,
    )
    gram = dot_nt(wide_in, wide_in, HIGHEST) * dot_nt(wide_out, wide_out, HIGHEST)
    spread = jnp.sum(jnp.where(same, gram, 0.0), axis=0, keepdims=True)
    token_sq = jnp.sum(jnp.where(same, spread, 0.0), axis=1, keepdims=True)
    scaled = (tgt_in * lax.rsqrt(token_sq[0:TOK] + 1e-06)).astype(BF16)
    low_out = tgt_out.astype(BF16)
    ids_low = ids_ref[...]
    for i in range(tmsg.shape[0]):
        tmsg[i, 0:TOK, :] = scaled
        tmsg[i, TOK : TOK + TOK // 2, :] = low_out
        tmsg[i, TOK + TOK // 2 : TMSG, :] = ids_low


def prepare(own, parts, ids, copies):
    return pl.pallas_call(
        prepare_kernel,
        out_shape=[
            jax.ShapeDtypeStruct((copies, TMSG, KH), BF16),
            jax.ShapeDtypeStruct((PMSG, KH), BF16),
            jax.ShapeDtypeStruct((8, ROWS), F32),
        ],
        compiler_params=pltpu.CompilerParams(vmem_limit_bytes=24 * MB),
        cost_estimate=pl.CostEstimate(flops=200_000_000, bytes_accessed=3_000_000, transcendentals=0),
        name="prepare",
    )(own, *parts, ids)


def score_kernel(last, t_ref, *refs):
    pools, refs = refs[:8], refs[8:]
    if last:
        tmsg, prev, scale, out, pin, pout, t_in, t_out, hot, best, rows = refs
    else:
        tmsg, out, pin, pout, t_in, t_out, hot, best, rows = refs
    half = ROWS // 2
    low = lane_mask((half, KH), True)
    for k, pool in enumerate(pools):
        pin[k * ROWS : (k + 1) * ROWS, :] = pool[0:ROWS, :]
        packed = pool[ROWS:PMSG, :].astype(F32)
        turned = pltpu.roll(packed, KG, 1)
        pout[k * ROWS : k * ROWS + half, :] = jnp.where(low, packed, turned).astype(BF16)
        pout[k * ROWS + half : (k + 1) * ROWS, :] = jnp.where(low, turned, packed).astype(BF16)
    best[...] = jnp.full(best.shape, -jnp.inf, F32)

    lane = lax.broadcasted_iota(jnp.int32, (1, KH), 1)
    keep_low = (lane < KG).astype(F32).astype(BF16)
    keep_high = (lane >= KG).astype(F32).astype(BF16)
    width = GROUP * TOK
    tile = 512
    example = lax.broadcasted_iota(jnp.int32, (GROUP * EX, KH), 0).astype(F32)

    def group(g, carry):
        for pair in range(GROUP // 2):
            b0 = g * GROUP + 2 * pair
            b1 = b0 + 1
            at = pair * 2 * TOK
            t_in[at : at + TOK, :] = tmsg[b0, 0:TOK, :]
            t_in[at + TOK : at + TOK + 64, :] = tmsg[b1, 128:TOK, :]
            t_in[at + TOK + 64 : at + 2 * TOK, :] = tmsg[b1, 0:128, :]
            o0 = tmsg[b0, TOK : TOK + 96, :]
            o1 = tmsg[b1, TOK : TOK + 96, :]
            t_out[at : at + 96, :] = o0 * keep_low
            t_out[at + 96 : at + TOK, :] = o0 * keep_high
            t_out[at + TOK : at + TOK + 64, :] = o1[32:96] * keep_high
            t_out[at + TOK + 64 : at + TOK + 160, :] = o1 * keep_low
            t_out[at + TOK + 160 : at + 2 * TOK, :] = o1[0:32] * keep_high
            i0 = tmsg[b0, TOK + 96 : TMSG, :].astype(F32) + float(2 * pair * EX)
            i1 = tmsg[b1, TOK + 96 : TMSG, :].astype(F32) + float((2 * pair + 1) * EX)
            mixed = jnp.where(lane < KG, i0[1:2, :], i1[1:2, :])
            hot[:, at : at + 128] = (example == i0[0:1, :]).astype(F32).astype(BF16)
            hot[:, at + 128 : at + 256] = (example == mixed).astype(F32).astype(BF16)
            hot[:, at + 256 : at + 384] = (example == i1[0:1, :]).astype(F32).astype(BF16)

        chunk = 512

        def rows_of(c, carry):
            at = pl.ds(pl.multiple_of(c * chunk, chunk), chunk)
            left_in = pin[at, :]
            left_out = pout[at, :]
            total = None
            for i in range(width // tile):
                cols = slice(i * tile, (i + 1) * tile)
                joined = dot_nt(left_in, t_in[cols, :]) * dot_nt(left_out, t_out[cols, :])
                part = dot_nt(joined.astype(BF16), hot[:, cols])
                total = part if total is None else total + part
            best[at, :] = jnp.maximum(best[at, :], total)
            return carry

        return lax.fori_loop(0, pin.shape[0] // chunk, rows_of, carry)

    lax.fori_loop(0, tmsg.shape[0] // GROUP, group, 0)
    t = t_ref[0]
    for k in range(8):
        row = jnp.max(best[k * ROWS : (k + 1) * ROWS, :].T, axis=0, keepdims=True)
        rows[pl.ds(lax.rem(t + 8 - k, 8), 1), :] = row
    if last:
        final = jnp.maximum(rows[...], prev[...])
        for i in range(out.shape[0]):
            out[i, 0:8, :] = final
            out[i, 8:16, :] = scale[...]
    else:
        out[...] = rows[...]


def score(t, pools, tmsg, *more):
    last = len(more) > 0
    width = GROUP * TOK
    shape = (8, 16, ROWS) if last else (8, ROWS)
    vmem = pl.BlockSpec(memory_space=pltpu.VMEM)
    return pl.pallas_call(
        functools.partial(score_kernel, last),
        in_specs=[pl.BlockSpec(memory_space=pltpu.SMEM)] + [vmem] * (9 + len(more)),
        out_specs=vmem,
        out_shape=jax.ShapeDtypeStruct(shape, F32),
        scratch_shapes=[
            pltpu.VMEM((8 * ROWS, KH), BF16),
            pltpu.VMEM((8 * ROWS, KH), BF16),
            pltpu.VMEM((width, KH), BF16),
            pltpu.VMEM((width, KH), BF16),
            pltpu.VMEM((GROUP * EX, width), BF16),
            pltpu.VMEM((8 * ROWS, GROUP * EX), F32),
            pltpu.VMEM((8, ROWS), F32),
        ],
        compiler_params=pltpu.CompilerParams(vmem_limit_bytes=24 * MB),
        cost_estimate=pl.CostEstimate(
            flops=5_000_000_000, bytes_accessed=2_000_000, transcendentals=0
        ),
        name="score_last" if last else "score_first",
    )(t[None], *pools, tmsg, *more)


def slots_kernel(t_ref, p_ref, got, owner, out):
    t = t_ref[0]
    first = (p_ref[0] * 8 + t) * ROWS
    best = got[0, 0:8, :]
    for i in range(1, 8):
        best = jnp.maximum(best, got[i, 0:8, :])
    sub = lax.broadcasted_iota(jnp.int32, (8, ROWS), 0)
    scale = jnp.zeros((8, ROWS), F32)
    for i in range(8):
        scale = jnp.where(sub == i, got[i, 8:16, :], scale)
    value = best * scale
    square = jnp.sum(value * value)
    mine = jnp.sum(jnp.where(sub == t, value, 0.0), axis=0, keepdims=True)

    across = jnp.broadcast_to(owner[...].astype(F32), (ROWS, ROWS))
    column = across.T
    row = lax.broadcasted_iota(jnp.int32, (ROWS, ROWS), 0)
    lane = lax.broadcasted_iota(jnp.int32, (ROWS, ROWS), 1)
    earlier = jnp.where((column == across) & (row < lane), 1.0, 0.0)
    rank = jnp.sum(earlier, axis=0, keepdims=True)
    number = (first + 1 + lax.broadcasted_iota(jnp.int32, (1, ROWS), 1)).astype(F32)
    owned = jnp.where(across[0:32] == row[0:32].astype(F32), 1.0, 0.0)
    slot = row.astype(F32)
    filled = jnp.where(slot == rank, mine, 0.0) + jnp.where(slot == rank + CAP, number, 0.0)
    placed = dot_nt(owned, jnp.where(row < 2 * CAP, filled, 0.0), HIGHEST)
    out[...] = jnp.where(lane[0:32] == 2 * CAP, square, placed)


def slots(t, p, got, owner):
    vmem = pl.BlockSpec(memory_space=pltpu.VMEM)
    smem = pl.BlockSpec(memory_space=pltpu.SMEM)
    return pl.pallas_call(
        slots_kernel,
        in_specs=[smem, smem, vmem, vmem],
        out_specs=vmem,
        out_shape=jax.ShapeDtypeStruct((32, ROWS), F32),
        compiler_params=pltpu.CompilerParams(vmem_limit_bytes=4 * MB),
        name="slots",
    )(t[None], p[None], got, owner)


def finish_kernel(tokens, got, weight, token):
    square = jnp.sum(got[:, 2 * CAP : 2 * CAP + 1])
    norm = lax.rsqrt(jnp.full((CAP, 32), square / tokens + 1e-06, F32))
    turned = jnp.concatenate([got[...], jnp.zeros((ROWS - 32, ROWS), F32)], axis=0).T
    weight[...] = turned[0:CAP, 0:32] * norm
    token[...] = turned[CAP : 2 * CAP, 0:32].astype(jnp.int32) - 1


def finish(got, tokens):
    return pl.pallas_call(
        functools.partial(finish_kernel, tokens),
        out_shape=[
            jax.ShapeDtypeStruct((CAP, 32), F32),
            jax.ShapeDtypeStruct((CAP, 32), jnp.int32),
        ],
        compiler_params=pltpu.CompilerParams(vmem_limit_bytes=4 * MB),
        name="finish",
    )(got)


def shift(x, axis, n, k):
    return lax.ppermute(x, axis, [(i, (i + k) % n) for i in range(n)])


def shards(ph, pg, th, tg, fin, fout, example, owner):
    n_tgt = lax.axis_size("tgt")
    n_pool = lax.axis_size("pool")
    t = lax.axis_index("tgt")
    p = lax.axis_index("pool")
    ids = jnp.zeros((16, KH), BF16)
    wide = example.astype(BF16)
    ids = ids.at[0:1, :].set(wide[:, 0:KH])
    ids = ids.at[1:2, :].set(jnp.concatenate([wide[:, KH:TOK]] * 2, axis=1))

    shared = (ph, pg, th, tg, fin, fout.T)
    after = lax.optimization_barrier
    up, down, opposite = project(
        LIMITS[0], t, (1, 7, 3, 5, 4), ((0, 0), (1, 0), (0, 1), (1, 1), (2, 0)), (BF16,) * 3, *shared
    )
    from_low = shift(up, "tgt", n_tgt, 1)
    from_high = shift(down, "tgt", n_tgt, n_tgt - 1)
    across = shift(opposite, "tgt", n_tgt, 4)
    t_next, up = after((t, up))
    two_up, two_down = project(LIMITS[1], t_next, (2, 6), ((0, 0), (1, 0)), (F32, F32), *shared)
    two_up, two_down = merge(from_low, from_high, two_up, two_down)
    t_next, two_up = after((t, two_up))
    from_low2 = shift(two_up, "tgt", n_tgt, 2)
    from_high2 = shift(two_down, "tgt", n_tgt, n_tgt - 2)
    (own,) = project(LIMITS[2], t_next, (0,), ((0, 0),), (F32,), *shared)
    parts = [from_low, from_high, across, from_low2, from_high2]
    tmsg, pmsg, scale = prepare(own, parts, ids, n_pool // 2)

    same_core = [[2 * i + c for i in range(n_pool // 2)] for c in range(2)]
    near = lax.all_to_all(
        tmsg, "pool", split_axis=0, concat_axis=0, tiled=True, axis_index_groups=same_core
    )
    pools = [pmsg] + [shift(pmsg, "tgt", n_tgt, k) for k in range(1, n_tgt)]
    near, *pools = after((near, *pools))
    far = lax.ppermute(near, "pool", [(i, i ^ 1) for i in range(n_pool)])
    partial = score(t, pools, near)
    best = score(t, pools, far, partial, scale)
    got = lax.all_to_all(best, "tgt", split_axis=0, concat_axis=0, tiled=True)
    sent = slots(t, p, got, owner.T)
    arrived = lax.all_to_all(sent, "pool", split_axis=0, concat_axis=0, tiled=True)
    weight, token = finish(arrived, float(n_pool * n_tgt * ROWS))
    return (weight.T[None, None], token.T[None, None])


def solution(mesh):
    rows = P("pool", "tgt")
    both = P(("pool", "tgt"), None)
    placed = (rows, rows, rows, rows, P("tgt", None), P("tgt", None), both, both)
    return jax.shard_map(
        shards,
        mesh=mesh,
        in_specs=placed,
        out_specs=(P("pool", "tgt", None, None), P("pool", "tgt", None, None)),
        check_vma=False,
    )
```

```python
import functools

import jax
import jax.numpy as jnp
from jax import lax
from jax.experimental import pallas as pl
from jax.experimental.pallas import tpu as pltpu
from jax.sharding import PartitionSpec as P

KH = 128
KG = 64
ROWS = 128
TOK = 192
EX = 16
CAP = 8
GROUP = 8
F32 = jnp.float32
BF16 = jnp.bfloat16
HIGHEST = lax.Precision.HIGHEST
MSG = ROWS + TOK + (ROWS + TOK) // 2
TMSG = TOK + TOK // 2 + 16
PMSG = ROWS + ROWS // 2
MB = 1024 * 1024
LIMITS = (60, 53, 53)


def dot_nt(a, b, precision=None):
    return lax.dot_general(
        a, b, (((1,), (1,)), ((), ())), preferred_element_type=F32, precision=precision
    )


def lane_mask(shape, low):
    lane = lax.broadcasted_iota(jnp.int32, shape, 1)
    return (lane < KG) if low else (lane >= KG)


def project_kernel(steps, kinds, t_ref, ph, pg, th, tg, fin, fout, *rest):
    outs, (rows_in, rows_out, fin_v, fout_v, sems) = rest[:-5], rest[-5:]
    t = t_ref[0]
    weights = [
        pltpu.make_async_copy(fout, fout_v, sems.at[0, 0]),
        pltpu.make_async_copy(fin, fin_v, sems.at[0, 1]),
    ]
    for copy in weights:
        copy.start()
    moves = []
    both = ROWS + TOK
    for i, k in enumerate(steps):
        who = lax.rem(t + k, 8)
        pool = pl.ds(pl.multiple_of(who * ROWS, ROWS), ROWS)
        tgt = pl.ds(pl.multiple_of(who * TOK, TOK), TOK)
        at_pool = pl.ds(i * both, ROWS)
        at_tgt = pl.ds(i * both + ROWS, TOK)
        here = [
            pltpu.make_async_copy(pg.at[pool, :], rows_out.at[at_pool, :], sems.at[i + 1, 0]),
            pltpu.make_async_copy(tg.at[tgt, :], rows_out.at[at_tgt, :], sems.at[i + 1, 1]),
            pltpu.make_async_copy(ph.at[pool, :], rows_in.at[at_pool, :], sems.at[i + 1, 2]),
            pltpu.make_async_copy(th.at[tgt, :], rows_in.at[at_tgt, :], sems.at[i + 1, 3]),
        ]
        for copy in here:
            copy.start()
        moves.append(here)
    for copy in weights:
        copy.wait()
    together = min(2, len(steps))
    for first in range(0, len(steps), together):
        count = min(together, len(steps) - first)
        for i in range(first, first + count):
            for copy in moves[i]:
                copy.wait()
        rows = slice(first * both, (first + count) * both)
        sums_out = dot_nt(rows_out[rows, :], fout_v[...])
        sums_in = jnp.dot(rows_in[rows, :], fin_v[...], preferred_element_type=F32)
        for i in range(first, first + count):
            lead = (i - first) * both
            message = [sums_in[lead : lead + both]]
            for size in (ROWS, TOK):
                half = size // 2
                message.append(
                    jnp.concatenate(
                        [sums_out[lead : lead + half], sums_out[lead + half : lead + size]], axis=1
                    )
                )
                lead = lead + size
            message = jnp.concatenate(message, axis=0)
            for which, at, start, stop in kinds[i]:
                out = outs[which]
                out[at : at + stop - start, :] = message[start:stop].astype(out.dtype)


def project(limit, t, steps, kinds, dtypes, ph, pg, th, tg, fin, fout):
    n = len(steps)
    pieces = [piece for kind in kinds for piece in kind]
    sizes = [sum(p[3] - p[2] for p in pieces if p[0] == j) for j in range(len(dtypes))]
    hbm = pl.BlockSpec(memory_space=pltpu.HBM)
    vmem = pl.BlockSpec(memory_space=pltpu.VMEM)
    return pl.pallas_call(
        functools.partial(project_kernel, steps, kinds),
        in_specs=[pl.BlockSpec(memory_space=pltpu.SMEM)] + [hbm] * 6,
        out_specs=[vmem for _ in dtypes],
        out_shape=[jax.ShapeDtypeStruct((c, KH), d) for c, d in zip(sizes, dtypes)],
        scratch_shapes=[
            pltpu.VMEM((n * (ROWS + TOK), ph.shape[1]), BF16),
            pltpu.VMEM((n * (ROWS + TOK), pg.shape[1]), BF16),
            pltpu.VMEM(fin.shape, BF16),
            pltpu.VMEM(fout.shape, BF16),
            pltpu.SemaphoreType.DMA((n + 1, 4)),
        ],
        compiler_params=pltpu.CompilerParams(vmem_limit_bytes=limit * MB),
        cost_estimate=pl.CostEstimate(
            flops=n * 170_000_000, bytes_accessed=n * 1_600_000, transcendentals=0
        ),
        name="project",
    )(t[None], ph, pg, th, tg, fin, fout)


def merge_kernel(from_low, from_high, half_low, half_high, mine_up, mine_down, up, down):
    half = MSG // 2
    total = mine_up[...] + from_low[MSG : 2 * MSG, :].astype(F32)
    up[0:half, :] = (total[0:half] + half_low[...].astype(F32)).astype(BF16)
    up[half:MSG, :] = total[half:MSG].astype(BF16)
    total = mine_down[...] + from_high[MSG : 2 * MSG, :].astype(F32)
    down[0:half, :] = total[0:half].astype(BF16)
    down[half:MSG, :] = (total[half:MSG] + half_high[...].astype(F32)).astype(BF16)


def merge(*operands):
    return pl.pallas_call(
        merge_kernel,
        out_shape=[jax.ShapeDtypeStruct((MSG, KH), BF16)] * 2,
        compiler_params=pltpu.CompilerParams(vmem_limit_bytes=8 * MB),
        cost_estimate=pl.CostEstimate(flops=200_000, bytes_accessed=1_500_000, transcendentals=0),
        name="merge",
    )(*operands)


def prepare_kernel(own, *rest):
    parts, (ids_ref, tmsg, pmsg, scale_ref, message, sems) = rest[:-6], rest[-6:]
    total = own[...]
    for part in parts:
        total = total + part[0:MSG, :].astype(F32)
    pool_in = total[0:ROWS]
    tgt_in = total[ROWS : ROWS + TOK]
    pool_out = total[ROWS + TOK : ROWS + TOK + ROWS // 2]
    tgt_out = total[ROWS + TOK + ROWS // 2 : MSG]

    ids = ids_ref[...].astype(F32)
    first = ids[0:1, :]
    second = jnp.where(lane_mask((1, KH), True), ids[1:2, :], -1.0)
    column = jnp.concatenate(
        [jnp.broadcast_to(first, (KH, KH)).T, jnp.broadcast_to(second, (KH, KH)).T], axis=0
    )
    same = jnp.concatenate([column == first, column == second], axis=1)
    pad = jnp.zeros((2 * KH - TOK, KH), F32)
    wide_in = jnp.concatenate([tgt_in, pad], axis=0)
    low = lane_mask(tgt_out.shape, True)
    zero = jnp.zeros_like(tgt_out)
    wide_out = jnp.concatenate(
        [
            jnp.where(low, tgt_out, zero),
            jnp.where(low, pltpu.roll(tgt_out, KG, 1), zero),
            pad,
        ],
        axis=0,
    )
    gram = dot_nt(wide_in, wide_in, HIGHEST) * dot_nt(wide_out, wide_out, HIGHEST)
    spread = jnp.sum(jnp.where(same, gram, 0.0), axis=0, keepdims=True)
    token_sq = jnp.sum(jnp.where(same, spread, 0.0), axis=1, keepdims=True)
    message[0:TOK, :] = (tgt_in * lax.rsqrt(token_sq[0:TOK] + 1e-06)).astype(BF16)
    message[TOK : TOK + TOK // 2, :] = tgt_out.astype(BF16)
    message[TOK + TOK // 2 : TMSG, :] = ids_ref[...]
    copies = [
        pltpu.make_async_copy(message, tmsg.at[i], sems.at[i]) for i in range(tmsg.shape[0])
    ]
    for copy in copies:
        copy.start()

    pmsg[0:ROWS, :] = pool_in.astype(BF16)
    pmsg[ROWS:PMSG, :] = pool_out.astype(BF16)
    low = lane_mask(pool_out.shape, True)
    zero = jnp.zeros_like(pool_out)
    out_rows = jnp.concatenate(
        [jnp.where(low, pool_out, zero), jnp.where(low, zero, pool_out)], axis=0
    )
    in_sq = jnp.sum((pool_in * pool_in).T, axis=0, keepdims=True)
    out_sq = jnp.sum((out_rows * out_rows).T, axis=0, keepdims=True)
    scale_ref[...] = jnp.broadcast_to(lax.rsqrt(in_sq * out_sq + 1e-06), scale_ref.shape)
    for copy in copies:
        copy.wait()


def prepare(own, parts, ids, copies):
    vmem = pl.BlockSpec(memory_space=pltpu.VMEM)
    return pl.pallas_call(
        prepare_kernel,
        out_specs=[pl.BlockSpec(memory_space=pl.ANY), vmem, vmem],
        out_shape=[
            jax.ShapeDtypeStruct((copies, TMSG, KH), BF16),
            jax.ShapeDtypeStruct((PMSG, KH), BF16),
            jax.ShapeDtypeStruct((8, ROWS), F32),
        ],
        scratch_shapes=[pltpu.VMEM((TMSG, KH), BF16), pltpu.SemaphoreType.DMA((copies,))],
        compiler_params=pltpu.CompilerParams(vmem_limit_bytes=24 * MB),
        cost_estimate=pl.CostEstimate(flops=200_000_000, bytes_accessed=3_000_000, transcendentals=0),
        name="prepare",
    )(own, *parts, ids)


def score_kernel(last, *refs):
    if last:
        t_ref, pin, pout, prev, tmsg, scale, out, t_in, t_out, hot, best, rows = refs
        best[...] = prev[...]
    else:
        pools, (tmsg, pin, pout, best, t_in, t_out, hot) = refs[:8], refs[8:]
        half = ROWS // 2
        low = lane_mask((half, KH), True)
        for k, pool in enumerate(pools):
            at = k * ROWS
            pin[at : at + ROWS, :] = pool[0:ROWS, :]
            packed = pool[ROWS:PMSG, :].astype(F32)
            turned = pltpu.roll(packed, KG, 1)
            pout[at : at + half, :] = jnp.where(low, packed, turned).astype(BF16)
            pout[at + half : at + ROWS, :] = jnp.where(low, turned, packed).astype(BF16)

    lane = lax.broadcasted_iota(jnp.int32, (1, KH), 1)
    keep_low = (lane < KG).astype(F32).astype(BF16)
    keep_high = (lane >= KG).astype(F32).astype(BF16)
    width = GROUP * TOK
    tile = 512
    example = lax.broadcasted_iota(jnp.int32, (GROUP * EX, KH), 0).astype(F32)

    groups = tmsg.shape[0] // GROUP
    for g in range(groups):
        for pair in range(GROUP // 2):
            b0 = g * GROUP + 2 * pair
            b1 = b0 + 1
            at = b0 * TOK
            t_in[at : at + TOK, :] = tmsg[b0, 0:TOK, :]
            t_in[at + TOK : at + TOK + 64, :] = tmsg[b1, 128:TOK, :]
            t_in[at + TOK + 64 : at + 2 * TOK, :] = tmsg[b1, 0:128, :]
            o0 = tmsg[b0, TOK : TOK + 96, :]
            o1 = tmsg[b1, TOK : TOK + 96, :]
            t_out[at : at + 96, :] = o0 * keep_low
            t_out[at + 96 : at + TOK, :] = o0 * keep_high
            t_out[at + TOK : at + TOK + 64, :] = o1[32:96] * keep_high
            t_out[at + TOK + 64 : at + TOK + 160, :] = o1 * keep_low
            t_out[at + TOK + 160 : at + 2 * TOK, :] = o1[0:32] * keep_high
            i0 = tmsg[b0, TOK + 96 : TMSG, :].astype(F32) + float(2 * pair * EX)
            i1 = tmsg[b1, TOK + 96 : TMSG, :].astype(F32) + float((2 * pair + 1) * EX)
            mixed = jnp.where(lane < KG, i0[1:2, :], i1[1:2, :])
            hot[:, at : at + 128] = (example == i0[0:1, :]).astype(F32).astype(BF16)
            hot[:, at + 128 : at + 256] = (example == mixed).astype(F32).astype(BF16)
            hot[:, at + 256 : at + 384] = (example == i1[0:1, :]).astype(F32).astype(BF16)
    for g in range(groups):
        total = None
        for i in range(width // tile):
            cols = slice(g * width + i * tile, g * width + (i + 1) * tile)
            joined = dot_nt(pin[...], t_in[cols, :]) * dot_nt(pout[...], t_out[cols, :])
            part = dot_nt(joined.astype(BF16), hot[:, cols])
            total = part if total is None else total + part
        if last or g:
            best[...] = jnp.maximum(best[...], total)
        else:
            best[...] = total
    if last:
        t = t_ref[0]
        for k in range(8):
            row = jnp.max(best[k * ROWS : (k + 1) * ROWS, :].T, axis=0, keepdims=True)
            rows[pl.ds(lax.rem(t + 8 - k, 8), 1), :] = row
        for i in range(out.shape[0]):
            out[i, 0:8, :] = rows[...]
            out[i, 8:16, :] = scale[...]


def score(last, *operands):
    tokens = operands[-2 if last else -1].shape[0] * TOK
    vmem = pl.BlockSpec(memory_space=pltpu.VMEM)
    smem = pl.BlockSpec(memory_space=pltpu.SMEM)
    unpacked = jax.ShapeDtypeStruct((8 * ROWS, KH), BF16)
    maxima = jax.ShapeDtypeStruct((8 * ROWS, GROUP * EX), F32)
    message = jax.ShapeDtypeStruct((8, 16, ROWS), F32)
    scratch = [
        pltpu.VMEM((tokens, KH), BF16),
        pltpu.VMEM((tokens, KH), BF16),
        pltpu.VMEM((GROUP * EX, tokens), BF16),
    ]
    if last:
        scratch += [pltpu.VMEM(maxima.shape, F32), pltpu.VMEM((8, ROWS), F32)]
    return pl.pallas_call(
        functools.partial(score_kernel, last),
        in_specs=[smem] * last + [vmem] * (len(operands) - last),
        out_specs=vmem if last else [vmem] * 3,
        out_shape=message if last else [unpacked, unpacked, maxima],
        scratch_shapes=scratch,
        compiler_params=pltpu.CompilerParams(vmem_limit_bytes=24 * MB),
        cost_estimate=pl.CostEstimate(
            flops=5_000_000_000, bytes_accessed=2_000_000, transcendentals=0
        ),
        name="score_last" if last else "score_first",
    )(*operands)


def slots_kernel(t_ref, p_ref, got, owner, out):
    t = t_ref[0]
    first = (p_ref[0] * 8 + t) * ROWS
    best = got[0, 0:8, :]
    for i in range(1, 8):
        best = jnp.maximum(best, got[i, 0:8, :])
    sub = lax.broadcasted_iota(jnp.int32, (8, ROWS), 0)
    scale = jnp.zeros((8, ROWS), F32)
    for i in range(8):
        scale = jnp.where(sub == i, got[i, 8:16, :], scale)
    value = best * scale
    square = jnp.sum(value * value)
    mine = jnp.sum(jnp.where(sub == t, value, 0.0), axis=0, keepdims=True)

    across = jnp.broadcast_to(owner[...].astype(F32), (ROWS, ROWS))
    column = across.T
    row = lax.broadcasted_iota(jnp.int32, (ROWS, ROWS), 0)
    lane = lax.broadcasted_iota(jnp.int32, (ROWS, ROWS), 1)
    earlier = jnp.where((column == across) & (row < lane), 1.0, 0.0)
    rank = jnp.sum(earlier, axis=0, keepdims=True)
    number = (first + 1 + lax.broadcasted_iota(jnp.int32, (1, ROWS), 1)).astype(F32)
    owned = jnp.where(across[0:32] == row[0:32].astype(F32), 1.0, 0.0)
    slot = row.astype(F32)
    filled = jnp.where(slot == rank, mine, 0.0) + jnp.where(slot == rank + CAP, number, 0.0)
    placed = dot_nt(owned, jnp.where(row < 2 * CAP, filled, 0.0), HIGHEST)
    out[...] = jnp.where(lane[0:32] == 2 * CAP, square, placed)


def slots(t, p, got, owner):
    vmem = pl.BlockSpec(memory_space=pltpu.VMEM)
    smem = pl.BlockSpec(memory_space=pltpu.SMEM)
    return pl.pallas_call(
        slots_kernel,
        in_specs=[smem, smem, vmem, vmem],
        out_specs=vmem,
        out_shape=jax.ShapeDtypeStruct((32, ROWS), F32),
        compiler_params=pltpu.CompilerParams(vmem_limit_bytes=4 * MB),
        name="slots",
    )(t[None], p[None], got, owner)


def finish_kernel(tokens, got, weight, token):
    square = jnp.sum(got[:, 2 * CAP : 2 * CAP + 1])
    norm = lax.rsqrt(jnp.full((CAP, 32), square / tokens + 1e-06, F32))
    turned = jnp.concatenate([got[...], jnp.zeros((ROWS - 32, ROWS), F32)], axis=0).T
    weight[...] = turned[0:CAP, 0:32] * norm
    token[...] = turned[CAP : 2 * CAP, 0:32].astype(jnp.int32) - 1


def finish(got, tokens):
    return pl.pallas_call(
        functools.partial(finish_kernel, tokens),
        out_shape=[
            jax.ShapeDtypeStruct((CAP, 32), F32),
            jax.ShapeDtypeStruct((CAP, 32), jnp.int32),
        ],
        compiler_params=pltpu.CompilerParams(vmem_limit_bytes=4 * MB),
        name="finish",
    )(got)


def shift(x, axis, n, k):
    return lax.ppermute(x, axis, [(i, (i + k) % n) for i in range(n)])


def shards(ph, pg, th, tg, fin, fout, example, owner):
    n_tgt = lax.axis_size("tgt")
    n_pool = lax.axis_size("pool")
    t = lax.axis_index("tgt")
    p = lax.axis_index("pool")
    ids = jnp.zeros((16, KH), BF16)
    wide = example.astype(BF16)
    ids = ids.at[0:1, :].set(wide[:, 0:KH])
    ids = ids.at[1:2, :].set(jnp.concatenate([wide[:, KH:TOK]] * 2, axis=1))

    shared = (ph, pg, th, tg, fin, fout.T)
    after = lax.optimization_barrier
    whole = lambda which, slot=0: ((which, slot * MSG, 0, MSG),)
    halves = ((2, 0, 0, MSG // 2), (3, 0, MSG // 2, MSG))
    up, down, opposite_up, opposite_down = project(
        LIMITS[0],
        t,
        (1, 7, 3, 5, 4),
        (whole(0), whole(1), whole(0, 1), whole(1, 1), halves),
        (BF16,) * 4,
        *shared,
    )
    from_low = shift(up, "tgt", n_tgt, 1)
    from_high = shift(down, "tgt", n_tgt, n_tgt - 1)
    half_low = shift(opposite_up, "tgt", n_tgt, 2)
    half_high = shift(opposite_down, "tgt", n_tgt, n_tgt - 2)
    t_next, up = after((t, up))
    two_up, two_down = project(
        LIMITS[1], t_next, (2, 6), (whole(0), whole(1)), (F32, F32), *shared
    )
    two_up, two_down = merge(from_low, from_high, half_low, half_high, two_up, two_down)
    t_next, two_up = after((t, two_up))
    from_low2 = shift(two_up, "tgt", n_tgt, 2)
    from_high2 = shift(two_down, "tgt", n_tgt, n_tgt - 2)
    (own,) = project(LIMITS[2], t_next, (0,), (whole(0),), (F32,), *shared)
    parts = [from_low, from_high, from_low2, from_high2]
    tmsg, pmsg, scale = prepare(own, parts, ids, n_pool // 2)

    same_core = [[2 * i + c for i in range(n_pool // 2)] for c in range(2)]
    near = lax.all_to_all(
        tmsg, "pool", split_axis=0, concat_axis=0, tiled=True, axis_index_groups=same_core
    )
    pools = [pmsg] + [shift(pmsg, "tgt", n_tgt, k) for k in range(1, n_tgt)]
    near, *pools = after((near, *pools))
    far = lax.ppermute(near, "pool", [(i, i ^ 1) for i in range(n_pool)])
    pin, pout, partial = score(False, *pools, near)
    best = score(True, t[None], pin, pout, partial, far, scale)
    got = lax.all_to_all(best, "tgt", split_axis=0, concat_axis=0, tiled=True)
    sent = slots(t, p, got, owner.T)
    arrived = lax.all_to_all(sent, "pool", split_axis=0, concat_axis=0, tiled=True)
    weight, token = finish(arrived, float(n_pool * n_tgt * ROWS))
    return (weight.T[None, None], token.T[None, None])


def solution(mesh):
    rows = P("pool", "tgt")
    both = P(("pool", "tgt"), None)
    placed = (rows, rows, rows, rows, P("tgt", None), P("tgt", None), both, both)
    return jax.shard_map(
        shards,
        mesh=mesh,
        in_specs=placed,
        out_specs=(P("pool", "tgt", None, None), P("pool", "tgt", None, None)),
        check_vma=False,
    )
```

```python
import functools

import jax
import jax.numpy as jnp
from jax import lax
from jax.experimental import pallas as pl
from jax.experimental.pallas import tpu as pltpu
from jax.sharding import PartitionSpec as P

KH = 128
KG = 64
ROWS = 128
TOK = 192
EX = 16
CAP = 8
GROUP = 8
F32 = jnp.float32
BF16 = jnp.bfloat16
HIGHEST = lax.Precision.HIGHEST
MSG = ROWS + TOK + (ROWS + TOK) // 2
TMSG = TOK + TOK // 2 + 16
PMSG = ROWS + ROWS // 2
MB = 1024 * 1024
LIMITS = (60, 53, 53)
POOL_ORDER = (7, 1, 6, 2, 5, 3, 4)


def dot_nt(a, b, precision=None):
    return lax.dot_general(
        a, b, (((1,), (1,)), ((), ())), preferred_element_type=F32, precision=precision
    )


def lane_mask(shape, low):
    lane = lax.broadcasted_iota(jnp.int32, shape, 1)
    return (lane < KG) if low else (lane >= KG)


def project_kernel(steps, kinds, t_ref, ph, pg, th, tg, fin, fout, *rest):
    outs, (rows_in, rows_out, fin_v, fout_v, sems) = rest[:-5], rest[-5:]
    t = t_ref[0]
    weights = [
        pltpu.make_async_copy(fout, fout_v, sems.at[0, 0]),
        pltpu.make_async_copy(fin, fin_v, sems.at[0, 1]),
    ]
    for copy in weights:
        copy.start()
    moves = []
    both = ROWS + TOK
    for i, k in enumerate(steps):
        who = lax.rem(t + k, 8)
        pool = pl.ds(pl.multiple_of(who * ROWS, ROWS), ROWS)
        tgt = pl.ds(pl.multiple_of(who * TOK, TOK), TOK)
        at_pool = pl.ds(i * both, ROWS)
        at_tgt = pl.ds(i * both + ROWS, TOK)
        here = [
            pltpu.make_async_copy(pg.at[pool, :], rows_out.at[at_pool, :], sems.at[i + 1, 0]),
            pltpu.make_async_copy(tg.at[tgt, :], rows_out.at[at_tgt, :], sems.at[i + 1, 1]),
            pltpu.make_async_copy(ph.at[pool, :], rows_in.at[at_pool, :], sems.at[i + 1, 2]),
            pltpu.make_async_copy(th.at[tgt, :], rows_in.at[at_tgt, :], sems.at[i + 1, 3]),
        ]
        for copy in here:
            copy.start()
        moves.append(here)
    for copy in weights:
        copy.wait()
    together = min(2, len(steps))
    for first in range(0, len(steps), together):
        count = min(together, len(steps) - first)
        for i in range(first, first + count):
            for copy in moves[i]:
                copy.wait()
        rows = slice(first * both, (first + count) * both)
        sums_out = dot_nt(rows_out[rows, :], fout_v[...])
        sums_in = jnp.dot(rows_in[rows, :], fin_v[...], preferred_element_type=F32)
        for i in range(first, first + count):
            lead = (i - first) * both
            message = [sums_in[lead : lead + both]]
            for size in (ROWS, TOK):
                half = size // 2
                message.append(
                    jnp.concatenate(
                        [sums_out[lead : lead + half], sums_out[lead + half : lead + size]], axis=1
                    )
                )
                lead = lead + size
            message = jnp.concatenate(message, axis=0)
            for which, at, start, stop in kinds[i]:
                out = outs[which]
                out[at : at + stop - start, :] = message[start:stop].astype(out.dtype)


def project(limit, t, steps, kinds, dtypes, ph, pg, th, tg, fin, fout):
    n = len(steps)
    pieces = [piece for kind in kinds for piece in kind]
    sizes = [sum(p[3] - p[2] for p in pieces if p[0] == j) for j in range(len(dtypes))]
    hbm = pl.BlockSpec(memory_space=pltpu.HBM)
    vmem = pl.BlockSpec(memory_space=pltpu.VMEM)
    return pl.pallas_call(
        functools.partial(project_kernel, steps, kinds),
        in_specs=[pl.BlockSpec(memory_space=pltpu.SMEM)] + [hbm] * 6,
        out_specs=[vmem for _ in dtypes],
        out_shape=[jax.ShapeDtypeStruct((c, KH), d) for c, d in zip(sizes, dtypes)],
        scratch_shapes=[
            pltpu.VMEM((n * (ROWS + TOK), ph.shape[1]), BF16),
            pltpu.VMEM((n * (ROWS + TOK), pg.shape[1]), BF16),
            pltpu.VMEM(fin.shape, BF16),
            pltpu.VMEM(fout.shape, BF16),
            pltpu.SemaphoreType.DMA((n + 1, 4)),
        ],
        compiler_params=pltpu.CompilerParams(vmem_limit_bytes=limit * MB),
        cost_estimate=pl.CostEstimate(
            flops=n * 170_000_000, bytes_accessed=n * 1_600_000, transcendentals=0
        ),
        name="project",
    )(t[None], ph, pg, th, tg, fin, fout)


def merge_kernel(from_low, from_high, half_low, half_high, mine_up, mine_down, up, down):
    half = MSG // 2
    total = mine_up[...] + from_low[MSG : 2 * MSG, :].astype(F32)
    up[0:half, :] = (total[0:half] + half_low[...].astype(F32)).astype(BF16)
    up[half:MSG, :] = total[half:MSG].astype(BF16)
    total = mine_down[...] + from_high[MSG : 2 * MSG, :].astype(F32)
    down[0:half, :] = total[0:half].astype(BF16)
    down[half:MSG, :] = (total[half:MSG] + half_high[...].astype(F32)).astype(BF16)


def merge(*operands):
    return pl.pallas_call(
        merge_kernel,
        out_shape=[jax.ShapeDtypeStruct((MSG, KH), BF16)] * 2,
        compiler_params=pltpu.CompilerParams(vmem_limit_bytes=8 * MB),
        cost_estimate=pl.CostEstimate(flops=200_000, bytes_accessed=1_500_000, transcendentals=0),
        name="merge",
    )(*operands)


def prepare_kernel(own, *rest):
    parts, (ids_ref, tmsg, pmsg, scale_ref, message, sems) = rest[:-6], rest[-6:]
    total = own[...]
    for part in parts:
        total = total + part[0:MSG, :].astype(F32)
    pool_in = total[0:ROWS]
    tgt_in = total[ROWS : ROWS + TOK]
    pool_out = total[ROWS + TOK : ROWS + TOK + ROWS // 2]
    tgt_out = total[ROWS + TOK + ROWS // 2 : MSG]

    ids = ids_ref[...].astype(F32)
    first = ids[0:1, :]
    second = jnp.where(lane_mask((1, KH), True), ids[1:2, :], -1.0)
    column = jnp.concatenate(
        [jnp.broadcast_to(first, (KH, KH)).T, jnp.broadcast_to(second, (KH, KH)).T], axis=0
    )
    same = jnp.concatenate([column == first, column == second], axis=1)
    pad = jnp.zeros((2 * KH - TOK, KH), F32)
    wide_in = jnp.concatenate([tgt_in, pad], axis=0)
    low = lane_mask(tgt_out.shape, True)
    zero = jnp.zeros_like(tgt_out)
    wide_out = jnp.concatenate(
        [
            jnp.where(low, tgt_out, zero),
            jnp.where(low, pltpu.roll(tgt_out, KG, 1), zero),
            pad,
        ],
        axis=0,
    )
    message[TOK : TOK + TOK // 2, :] = tgt_out.astype(BF16)
    message[TOK + TOK // 2 : TMSG, :] = ids_ref[...]
    copies = []
    for i in range(tmsg.shape[0]):
        for j, rows in enumerate((slice(TOK, TMSG), slice(0, TOK))):
            here, there = message.at[rows, :], tmsg.at[i, rows, :]
            copies.append(pltpu.make_async_copy(here, there, sems.at[i, j]))
    for copy in copies[0::2]:
        copy.start()
    gram = dot_nt(wide_in, wide_in, HIGHEST) * dot_nt(wide_out, wide_out, HIGHEST)
    spread = jnp.sum(jnp.where(same, gram, 0.0), axis=0, keepdims=True)
    token_sq = jnp.sum(jnp.where(same, spread, 0.0), axis=1, keepdims=True)
    message[0:TOK, :] = (tgt_in * lax.rsqrt(token_sq[0:TOK] + 1e-06)).astype(BF16)
    for copy in copies[1::2]:
        copy.start()

    pmsg[0:ROWS, :] = pool_in.astype(BF16)
    pmsg[ROWS:PMSG, :] = pool_out.astype(BF16)
    low = lane_mask(pool_out.shape, True)
    zero = jnp.zeros_like(pool_out)
    out_rows = jnp.concatenate(
        [jnp.where(low, pool_out, zero), jnp.where(low, zero, pool_out)], axis=0
    )
    in_sq = jnp.sum((pool_in * pool_in).T, axis=0, keepdims=True)
    out_sq = jnp.sum((out_rows * out_rows).T, axis=0, keepdims=True)
    scale_ref[...] = jnp.broadcast_to(lax.rsqrt(in_sq * out_sq + 1e-06), scale_ref.shape)
    for copy in copies:
        copy.wait()


def prepare(own, parts, ids, copies):
    vmem = pl.BlockSpec(memory_space=pltpu.VMEM)
    return pl.pallas_call(
        prepare_kernel,
        out_specs=[pl.BlockSpec(memory_space=pl.ANY), vmem, vmem],
        out_shape=[
            jax.ShapeDtypeStruct((copies, TMSG, KH), BF16),
            jax.ShapeDtypeStruct((PMSG, KH), BF16),
            jax.ShapeDtypeStruct((8, ROWS), F32),
        ],
        scratch_shapes=[pltpu.VMEM((TMSG, KH), BF16), pltpu.SemaphoreType.DMA((copies, 2))],
        compiler_params=pltpu.CompilerParams(vmem_limit_bytes=24 * MB),
        cost_estimate=pl.CostEstimate(flops=200_000_000, bytes_accessed=3_000_000, transcendentals=0),
        name="prepare",
    )(own, *parts, ids)


def score_kernel(last, *refs):
    if last:
        t_ref, pin, pout, prev, tmsg, scale, out, t_in, t_out, hot, best, rows = refs
        best[...] = prev[...]
    else:
        pools, (tmsg, pin, pout, best, t_in, t_out, hot) = refs[:8], refs[8:]
        half = ROWS // 2
        low = lane_mask((half, KH), True)
        for k, pool in zip((0,) + POOL_ORDER, pools):
            at = k * ROWS
            pin[at : at + ROWS, :] = pool[0:ROWS, :]
            packed = pool[ROWS:PMSG, :].astype(F32)
            turned = pltpu.roll(packed, KG, 1)
            pout[at : at + half, :] = jnp.where(low, packed, turned).astype(BF16)
            pout[at + half : at + ROWS, :] = jnp.where(low, turned, packed).astype(BF16)

    lane = lax.broadcasted_iota(jnp.int32, (1, KH), 1)
    keep_low = (lane < KG).astype(F32).astype(BF16)
    keep_high = (lane >= KG).astype(F32).astype(BF16)
    width = GROUP * TOK
    tile = 512
    example = lax.broadcasted_iota(jnp.int32, (GROUP * EX, KH), 0).astype(F32)

    groups = tmsg.shape[0] // GROUP
    for g in range(groups):
        for pair in range(GROUP // 2):
            b0 = g * GROUP + 2 * pair
            b1 = b0 + 1
            at = b0 * TOK
            t_in[at : at + TOK, :] = tmsg[b0, 0:TOK, :]
            t_in[at + TOK : at + TOK + 64, :] = tmsg[b1, 128:TOK, :]
            t_in[at + TOK + 64 : at + 2 * TOK, :] = tmsg[b1, 0:128, :]
            o0 = tmsg[b0, TOK : TOK + 96, :]
            o1 = tmsg[b1, TOK : TOK + 96, :]
            t_out[at : at + 96, :] = o0 * keep_low
            t_out[at + 96 : at + TOK, :] = o0 * keep_high
            t_out[at + TOK : at + TOK + 64, :] = o1[32:96] * keep_high
            t_out[at + TOK + 64 : at + TOK + 160, :] = o1 * keep_low
            t_out[at + TOK + 160 : at + 2 * TOK, :] = o1[0:32] * keep_high
            i0 = tmsg[b0, TOK + 96 : TMSG, :].astype(F32) + float(2 * pair * EX)
            i1 = tmsg[b1, TOK + 96 : TMSG, :].astype(F32) + float((2 * pair + 1) * EX)
            mixed = jnp.where(lane < KG, i0[1:2, :], i1[1:2, :])
            hot[:, at : at + 128] = (example == i0[0:1, :]).astype(F32).astype(BF16)
            hot[:, at + 128 : at + 256] = (example == mixed).astype(F32).astype(BF16)
            hot[:, at + 256 : at + 384] = (example == i1[0:1, :]).astype(F32).astype(BF16)
    for g in range(groups):
        total = None
        for i in range(width // tile):
            cols = slice(g * width + i * tile, g * width + (i + 1) * tile)
            joined = dot_nt(pin[...], t_in[cols, :]) * dot_nt(pout[...], t_out[cols, :])
            part = dot_nt(joined.astype(BF16), hot[:, cols])
            total = part if total is None else total + part
        if last or g:
            best[...] = jnp.maximum(best[...], total)
        else:
            best[...] = total
    if last:
        t = t_ref[0]
        for k in range(8):
            row = jnp.max(best[k * ROWS : (k + 1) * ROWS, :].T, axis=0, keepdims=True)
            rows[pl.ds(lax.rem(t + 8 - k, 8), 1), :] = row
        for i in range(out.shape[0]):
            out[i, 0:8, :] = rows[...]
            out[i, 8:16, :] = scale[...]


def score(last, *operands):
    tokens = operands[-2 if last else -1].shape[0] * TOK
    vmem = pl.BlockSpec(memory_space=pltpu.VMEM)
    smem = pl.BlockSpec(memory_space=pltpu.SMEM)
    unpacked = jax.ShapeDtypeStruct((8 * ROWS, KH), BF16)
    maxima = jax.ShapeDtypeStruct((8 * ROWS, GROUP * EX), F32)
    message = jax.ShapeDtypeStruct((8, 16, ROWS), F32)
    scratch = [
        pltpu.VMEM((tokens, KH), BF16),
        pltpu.VMEM((tokens, KH), BF16),
        pltpu.VMEM((GROUP * EX, tokens), BF16),
    ]
    if last:
        scratch += [pltpu.VMEM(maxima.shape, F32), pltpu.VMEM((8, ROWS), F32)]
    return pl.pallas_call(
        functools.partial(score_kernel, last),
        in_specs=[smem] * last + [vmem] * (len(operands) - last),
        out_specs=vmem if last else [vmem] * 3,
        out_shape=message if last else [unpacked, unpacked, maxima],
        scratch_shapes=scratch,
        compiler_params=pltpu.CompilerParams(vmem_limit_bytes=24 * MB),
        cost_estimate=pl.CostEstimate(
            flops=5_000_000_000, bytes_accessed=2_000_000, transcendentals=0
        ),
        name="score_last" if last else "score_first",
    )(*operands)


def slots_kernel(t_ref, p_ref, got, owner, out):
    t = t_ref[0]
    first = (p_ref[0] * 8 + t) * ROWS
    best = got[0, 0:8, :]
    for i in range(1, 8):
        best = jnp.maximum(best, got[i, 0:8, :])
    sub = lax.broadcasted_iota(jnp.int32, (8, ROWS), 0)
    scale = jnp.zeros((8, ROWS), F32)
    for i in range(8):
        scale = jnp.where(sub == i, got[i, 8:16, :], scale)
    value = best * scale
    square = jnp.sum(value * value)
    mine = jnp.sum(jnp.where(sub == t, value, 0.0), axis=0, keepdims=True)

    across = jnp.broadcast_to(owner[...].astype(F32), (ROWS, ROWS))
    column = across.T
    row = lax.broadcasted_iota(jnp.int32, (ROWS, ROWS), 0)
    lane = lax.broadcasted_iota(jnp.int32, (ROWS, ROWS), 1)
    earlier = jnp.where((column == across) & (row < lane), 1.0, 0.0)
    rank = jnp.sum(earlier, axis=0, keepdims=True)
    number = (first + 1 + lax.broadcasted_iota(jnp.int32, (1, ROWS), 1)).astype(F32)
    owned = jnp.where(across[0:32] == row[0:32].astype(F32), 1.0, 0.0)
    slot = row.astype(F32)
    filled = jnp.where(slot == rank, mine, 0.0) + jnp.where(slot == rank + CAP, number, 0.0)
    placed = dot_nt(owned, jnp.where(row < 2 * CAP, filled, 0.0), HIGHEST)
    out[...] = jnp.where(lane[0:32] == 2 * CAP, square, placed)


def slots(t, p, got, owner):
    vmem = pl.BlockSpec(memory_space=pltpu.VMEM)
    smem = pl.BlockSpec(memory_space=pltpu.SMEM)
    return pl.pallas_call(
        slots_kernel,
        in_specs=[smem, smem, vmem, vmem],
        out_specs=vmem,
        out_shape=jax.ShapeDtypeStruct((32, ROWS), F32),
        compiler_params=pltpu.CompilerParams(vmem_limit_bytes=4 * MB),
        name="slots",
    )(t[None], p[None], got, owner)


def finish_kernel(tokens, got, weight, token):
    square = jnp.sum(got[:, 2 * CAP : 2 * CAP + 1])
    norm = lax.rsqrt(jnp.full((CAP, 32), square / tokens + 1e-06, F32))
    turned = jnp.concatenate([got[...], jnp.zeros((ROWS - 32, ROWS), F32)], axis=0).T
    weight[...] = turned[0:CAP, 0:32] * norm
    token[...] = turned[CAP : 2 * CAP, 0:32].astype(jnp.int32) - 1


def finish(got, tokens):
    return pl.pallas_call(
        functools.partial(finish_kernel, tokens),
        out_shape=[
            jax.ShapeDtypeStruct((CAP, 32), F32),
            jax.ShapeDtypeStruct((CAP, 32), jnp.int32),
        ],
        compiler_params=pltpu.CompilerParams(vmem_limit_bytes=4 * MB),
        name="finish",
    )(got)


def shift(x, axis, n, k):
    return lax.ppermute(x, axis, [(i, (i + k) % n) for i in range(n)])


def shards(ph, pg, th, tg, fin, fout, example, owner):
    n_tgt = lax.axis_size("tgt")
    n_pool = lax.axis_size("pool")
    t = lax.axis_index("tgt")
    p = lax.axis_index("pool")
    ids = jnp.zeros((16, KH), BF16)
    wide = example.astype(BF16)
    ids = ids.at[0:1, :].set(wide[:, 0:KH])
    ids = ids.at[1:2, :].set(jnp.concatenate([wide[:, KH:TOK]] * 2, axis=1))

    shared = (ph, pg, th, tg, fin, fout.T)
    after = lax.optimization_barrier
    whole = lambda which, slot=0: ((which, slot * MSG, 0, MSG),)
    halves = ((2, 0, 0, MSG // 2), (3, 0, MSG // 2, MSG))
    up, down, opposite_up, opposite_down = project(
        LIMITS[0],
        t,
        (1, 7, 3, 5, 4),
        (whole(0), whole(1), whole(0, 1), whole(1, 1), halves),
        (BF16,) * 4,
        *shared,
    )
    from_low = shift(up, "tgt", n_tgt, 1)
    from_high = shift(down, "tgt", n_tgt, n_tgt - 1)
    half_low = shift(opposite_up, "tgt", n_tgt, 2)
    half_high = shift(opposite_down, "tgt", n_tgt, n_tgt - 2)
    t_next, up = after((t, up))
    two_up, two_down = project(
        LIMITS[1], t_next, (2, 6), (whole(0), whole(1)), (F32, F32), *shared
    )
    two_up, two_down = merge(from_low, from_high, half_low, half_high, two_up, two_down)
    t_next, two_up = after((t, two_up))
    from_low2 = shift(two_up, "tgt", n_tgt, 2)
    from_high2 = shift(two_down, "tgt", n_tgt, n_tgt - 2)
    (own,) = project(LIMITS[2], t_next, (0,), (whole(0),), (F32,), *shared)
    parts = [from_low, from_high, from_low2, from_high2]
    tmsg, pmsg, scale = prepare(own, parts, ids, n_pool // 2)

    same_core = [[2 * i + c for i in range(n_pool // 2)] for c in range(2)]
    near = lax.all_to_all(
        tmsg, "pool", split_axis=0, concat_axis=0, tiled=True, axis_index_groups=same_core
    )
    pools = [pmsg] + [shift(pmsg, "tgt", n_tgt, k) for k in POOL_ORDER]
    near, *pools = after((near, *pools))
    far = lax.ppermute(near, "pool", [(i, i ^ 1) for i in range(n_pool)])
    pin, pout, partial = score(False, *pools, near)
    best = score(True, t[None], pin, pout, partial, far, scale)
    got = lax.all_to_all(best, "tgt", split_axis=0, concat_axis=0, tiled=True)
    sent = slots(t, p, got, owner.T)
    arrived = lax.all_to_all(sent, "pool", split_axis=0, concat_axis=0, tiled=True)
    weight, token = finish(arrived, float(n_pool * n_tgt * ROWS))
    return (weight.T[None, None], token.T[None, None])


def solution(mesh):
    rows = P("pool", "tgt")
    both = P(("pool", "tgt"), None)
    placed = (rows, rows, rows, rows, P("tgt", None), P("tgt", None), both, both)
    return jax.shard_map(
        shards,
        mesh=mesh,
        in_specs=placed,
        out_specs=(P("pool", "tgt", None, None), P("pool", "tgt", None, None)),
        check_vma=False,
    )
```

```python
import functools

import jax
import jax.numpy as jnp
from jax import lax
from jax.experimental import pallas as pl
from jax.experimental.pallas import tpu as pltpu
from jax.sharding import PartitionSpec as P

KH = 128
KG = 64
ROWS = 128
TOK = 192
EX = 16
CAP = 8
GROUP = 8
F32 = jnp.float32
BF16 = jnp.bfloat16
HIGHEST = lax.Precision.HIGHEST
MSG = ROWS + TOK + (ROWS + TOK) // 2
TMSG = TOK + TOK // 2 + 16
PMSG = ROWS + ROWS // 2
MB = 1024 * 1024
LIMITS = (60, 53, 53)
POOL_ORDER = (7, 1, 6, 2, 4, 5, 3)


def dot_nt(a, b, precision=None):
    return lax.dot_general(
        a, b, (((1,), (1,)), ((), ())), preferred_element_type=F32, precision=precision
    )


def lane_mask(shape, low):
    lane = lax.broadcasted_iota(jnp.int32, shape, 1)
    return (lane < KG) if low else (lane >= KG)


def project_kernel(steps, kinds, t_ref, ph, pg, th, tg, fin, fout, *rest):
    outs, (rows_in, rows_out, fin_v, fout_v, sems) = rest[:-5], rest[-5:]
    t = t_ref[0]
    weights = [
        pltpu.make_async_copy(fout, fout_v, sems.at[0, 0]),
        pltpu.make_async_copy(fin, fin_v, sems.at[0, 1]),
    ]
    for copy in weights:
        copy.start()
    moves = []
    both = ROWS + TOK
    for i, k in enumerate(steps):
        who = lax.rem(t + k, 8)
        pool = pl.ds(pl.multiple_of(who * ROWS, ROWS), ROWS)
        tgt = pl.ds(pl.multiple_of(who * TOK, TOK), TOK)
        at_pool = pl.ds(i * both, ROWS)
        at_tgt = pl.ds(i * both + ROWS, TOK)
        here = [
            pltpu.make_async_copy(pg.at[pool, :], rows_out.at[at_pool, :], sems.at[i + 1, 0]),
            pltpu.make_async_copy(tg.at[tgt, :], rows_out.at[at_tgt, :], sems.at[i + 1, 1]),
            pltpu.make_async_copy(ph.at[pool, :], rows_in.at[at_pool, :], sems.at[i + 1, 2]),
            pltpu.make_async_copy(th.at[tgt, :], rows_in.at[at_tgt, :], sems.at[i + 1, 3]),
        ]
        for copy in here:
            copy.start()
        moves.append(here)
    for copy in weights:
        copy.wait()
    together = len(steps)
    for first in range(0, len(steps), together):
        count = min(together, len(steps) - first)
        for i in range(first, first + count):
            for copy in moves[i]:
                copy.wait()
        rows = slice(first * both, (first + count) * both)
        sums_out = dot_nt(rows_out[rows, :], fout_v[...])
        sums_in = jnp.dot(rows_in[rows, :], fin_v[...], preferred_element_type=F32)
        for i in range(first, first + count):
            lead = (i - first) * both
            message = [sums_in[lead : lead + both]]
            for size in (ROWS, TOK):
                half = size // 2
                message.append(
                    jnp.concatenate(
                        [sums_out[lead : lead + half], sums_out[lead + half : lead + size]], axis=1
                    )
                )
                lead = lead + size
            message = jnp.concatenate(message, axis=0)
            for which, at, start, stop in kinds[i]:
                out = outs[which]
                out[at : at + stop - start, :] = message[start:stop].astype(out.dtype)


def project(limit, t, steps, kinds, dtypes, ph, pg, th, tg, fin, fout):
    n = len(steps)
    pieces = [piece for kind in kinds for piece in kind]
    sizes = [sum(p[3] - p[2] for p in pieces if p[0] == j) for j in range(len(dtypes))]
    hbm = pl.BlockSpec(memory_space=pltpu.HBM)
    vmem = pl.BlockSpec(memory_space=pltpu.VMEM)
    return pl.pallas_call(
        functools.partial(project_kernel, steps, kinds),
        in_specs=[pl.BlockSpec(memory_space=pltpu.SMEM)] + [hbm] * 6,
        out_specs=[vmem for _ in dtypes],
        out_shape=[jax.ShapeDtypeStruct((c, KH), d) for c, d in zip(sizes, dtypes)],
        scratch_shapes=[
            pltpu.VMEM((n * (ROWS + TOK), ph.shape[1]), BF16),
            pltpu.VMEM((n * (ROWS + TOK), pg.shape[1]), BF16),
            pltpu.VMEM(fin.shape, BF16),
            pltpu.VMEM(fout.shape, BF16),
            pltpu.SemaphoreType.DMA((n + 1, 4)),
        ],
        compiler_params=pltpu.CompilerParams(vmem_limit_bytes=limit * MB),
        cost_estimate=pl.CostEstimate(
            flops=n * 170_000_000, bytes_accessed=n * 1_600_000, transcendentals=0
        ),
        name="project",
    )(t[None], ph, pg, th, tg, fin, fout)


def merge_kernel(from_low, from_high, half_low, half_high, mine_up, mine_down, up, down):
    half = MSG // 2
    total = mine_up[...] + from_low[MSG : 2 * MSG, :].astype(F32)
    up[0:half, :] = (total[0:half] + half_low[...].astype(F32)).astype(BF16)
    up[half:MSG, :] = total[half:MSG].astype(BF16)
    total = mine_down[...] + from_high[MSG : 2 * MSG, :].astype(F32)
    down[0:half, :] = total[0:half].astype(BF16)
    down[half:MSG, :] = (total[half:MSG] + half_high[...].astype(F32)).astype(BF16)


def merge(*operands):
    return pl.pallas_call(
        merge_kernel,
        out_shape=[jax.ShapeDtypeStruct((MSG, KH), BF16)] * 2,
        compiler_params=pltpu.CompilerParams(vmem_limit_bytes=8 * MB),
        cost_estimate=pl.CostEstimate(flops=200_000, bytes_accessed=1_500_000, transcendentals=0),
        name="merge",
    )(*operands)


def prepare_kernel(own, *rest):
    parts, (ids_ref, tmsg, pmsg, scale_ref, message, sems) = rest[:-6], rest[-6:]
    total = own[...]
    for part in parts:
        total = total + part[0:MSG, :].astype(F32)
    pool_in = total[0:ROWS]
    tgt_in = total[ROWS : ROWS + TOK]
    pool_out = total[ROWS + TOK : ROWS + TOK + ROWS // 2]
    tgt_out = total[ROWS + TOK + ROWS // 2 : MSG]

    ids = ids_ref[...].astype(F32)
    first = ids[0:1, :]
    second = jnp.where(lane_mask((1, KH), True), ids[1:2, :], -1.0)
    column = jnp.concatenate(
        [jnp.broadcast_to(first, (KH, KH)).T, jnp.broadcast_to(second, (KH, KH)).T], axis=0
    )
    same = jnp.concatenate([column == first, column == second], axis=1)
    pad = jnp.zeros((2 * KH - TOK, KH), F32)
    wide_in = jnp.concatenate([tgt_in, pad], axis=0)
    low = lane_mask(tgt_out.shape, True)
    zero = jnp.zeros_like(tgt_out)
    wide_out = jnp.concatenate(
        [
            jnp.where(low, tgt_out, zero),
            jnp.where(low, pltpu.roll(tgt_out, KG, 1), zero),
            pad,
        ],
        axis=0,
    )
    message[TOK : TOK + TOK // 2, :] = tgt_out.astype(BF16)
    message[TOK + TOK // 2 : TMSG, :] = ids_ref[...]
    copies = []
    for i in range(tmsg.shape[0]):
        for j, rows in enumerate((slice(TOK, TMSG), slice(0, TOK))):
            here, there = message.at[rows, :], tmsg.at[i, rows, :]
            copies.append(pltpu.make_async_copy(here, there, sems.at[i, j]))
    for copy in copies[0::2]:
        copy.start()
    gram = dot_nt(wide_in, wide_in, HIGHEST) * dot_nt(wide_out, wide_out, HIGHEST)
    spread = jnp.sum(jnp.where(same, gram, 0.0), axis=0, keepdims=True)
    token_sq = jnp.sum(jnp.where(same, spread, 0.0), axis=1, keepdims=True)
    message[0:TOK, :] = (tgt_in * lax.rsqrt(token_sq[0:TOK] + 1e-06)).astype(BF16)
    for copy in copies[1::2]:
        copy.start()

    pmsg[0:ROWS, :] = pool_in.astype(BF16)
    pmsg[ROWS:PMSG, :] = pool_out.astype(BF16)
    low = lane_mask(pool_out.shape, True)
    zero = jnp.zeros_like(pool_out)
    out_rows = jnp.concatenate(
        [jnp.where(low, pool_out, zero), jnp.where(low, zero, pool_out)], axis=0
    )
    in_sq = jnp.sum((pool_in * pool_in).T, axis=0, keepdims=True)
    out_sq = jnp.sum((out_rows * out_rows).T, axis=0, keepdims=True)
    scale_ref[...] = jnp.broadcast_to(lax.rsqrt(in_sq * out_sq + 1e-06), scale_ref.shape)
    for copy in copies:
        copy.wait()


def prepare(own, parts, ids, copies):
    vmem = pl.BlockSpec(memory_space=pltpu.VMEM)
    return pl.pallas_call(
        prepare_kernel,
        out_specs=[pl.BlockSpec(memory_space=pl.ANY), vmem, vmem],
        out_shape=[
            jax.ShapeDtypeStruct((copies, TMSG, KH), BF16),
            jax.ShapeDtypeStruct((PMSG, KH), BF16),
            jax.ShapeDtypeStruct((8, ROWS), F32),
        ],
        scratch_shapes=[pltpu.VMEM((TMSG, KH), BF16), pltpu.SemaphoreType.DMA((copies, 2))],
        compiler_params=pltpu.CompilerParams(vmem_limit_bytes=24 * MB),
        cost_estimate=pl.CostEstimate(flops=200_000_000, bytes_accessed=3_000_000, transcendentals=0),
        name="prepare",
    )(own, *parts, ids)


def score_kernel(last, *refs):
    if last:
        t_ref, pin, pout, prev, tmsg, scale, out, t_in, t_out, hot, best, rows = refs
    else:
        pools, (tmsg, pin, pout, best, t_in, t_out, hot) = refs[:8], refs[8:]
        half = ROWS // 2
        low = lane_mask((half, KH), True)
        for k, pool in zip((0,) + POOL_ORDER, pools):
            at = k * ROWS
            pin[at : at + ROWS, :] = pool[0:ROWS, :]
            packed = pool[ROWS:PMSG, :].astype(F32)
            turned = pltpu.roll(packed, KG, 1)
            pout[at : at + half, :] = jnp.where(low, packed, turned).astype(BF16)
            pout[at + half : at + ROWS, :] = jnp.where(low, turned, packed).astype(BF16)

    lane = lax.broadcasted_iota(jnp.int32, (1, KH), 1)
    keep_low = (lane < KG).astype(F32).astype(BF16)
    keep_high = (lane >= KG).astype(F32).astype(BF16)
    width = GROUP * TOK
    tile = 512
    example = lax.broadcasted_iota(jnp.int32, (GROUP * EX, KH), 0).astype(F32)

    groups = tmsg.shape[0] // GROUP
    for g in range(groups):
        for pair in range(GROUP // 2):
            b0 = g * GROUP + 2 * pair
            b1 = b0 + 1
            at = b0 * TOK
            t_in[at : at + TOK, :] = tmsg[b0, 0:TOK, :]
            t_in[at + TOK : at + TOK + 64, :] = tmsg[b1, 128:TOK, :]
            t_in[at + TOK + 64 : at + 2 * TOK, :] = tmsg[b1, 0:128, :]
            o0 = tmsg[b0, TOK : TOK + 96, :]
            o1 = tmsg[b1, TOK : TOK + 96, :]
            t_out[at : at + 96, :] = o0 * keep_low
            t_out[at + 96 : at + TOK, :] = o0 * keep_high
            t_out[at + TOK : at + TOK + 64, :] = o1[32:96] * keep_high
            t_out[at + TOK + 64 : at + TOK + 160, :] = o1 * keep_low
            t_out[at + TOK + 160 : at + 2 * TOK, :] = o1[0:32] * keep_high
            i0 = tmsg[b0, TOK + 96 : TMSG, :].astype(F32) + float(2 * pair * EX)
            i1 = tmsg[b1, TOK + 96 : TMSG, :].astype(F32) + float((2 * pair + 1) * EX)
            mixed = jnp.where(lane < KG, i0[1:2, :], i1[1:2, :])
            hot[:, at : at + 128] = (example == i0[0:1, :]).astype(F32).astype(BF16)
            hot[:, at + 128 : at + 256] = (example == mixed).astype(F32).astype(BF16)
            hot[:, at + 256 : at + 384] = (example == i1[0:1, :]).astype(F32).astype(BF16)
    for g in range(groups):
        total = None
        for i in range(width // tile):
            cols = slice(g * width + i * tile, g * width + (i + 1) * tile)
            joined = dot_nt(pin[...], t_in[cols, :]) * dot_nt(pout[...], t_out[cols, :])
            part = dot_nt(joined.astype(BF16), hot[:, cols])
            total = part if total is None else total + part
        if last or g:
            so_far = best if g else prev
            best[...] = jnp.maximum(so_far[...], total)
        else:
            best[...] = total
    if last:
        t = t_ref[0]
        for k in range(8):
            row = jnp.max(best[k * ROWS : (k + 1) * ROWS, :].T, axis=0, keepdims=True)
            rows[pl.ds(lax.rem(t + 8 - k, 8), 1), :] = row
        for i in range(out.shape[0]):
            out[i, 0:8, :] = rows[...]
            out[i, 8:16, :] = scale[...]


def score(last, *operands):
    tokens = operands[-2 if last else -1].shape[0] * TOK
    vmem = pl.BlockSpec(memory_space=pltpu.VMEM)
    smem = pl.BlockSpec(memory_space=pltpu.SMEM)
    unpacked = jax.ShapeDtypeStruct((8 * ROWS, KH), BF16)
    maxima = jax.ShapeDtypeStruct((8 * ROWS, GROUP * EX), F32)
    message = jax.ShapeDtypeStruct((8, 16, ROWS), F32)
    scratch = [
        pltpu.VMEM((tokens, KH), BF16),
        pltpu.VMEM((tokens, KH), BF16),
        pltpu.VMEM((GROUP * EX, tokens), BF16),
    ]
    if last:
        scratch += [pltpu.VMEM(maxima.shape, F32), pltpu.VMEM((8, ROWS), F32)]
    return pl.pallas_call(
        functools.partial(score_kernel, last),
        in_specs=[smem] * last + [vmem] * (len(operands) - last),
        out_specs=vmem if last else [vmem] * 3,
        out_shape=message if last else [unpacked, unpacked, maxima],
        scratch_shapes=scratch,
        compiler_params=pltpu.CompilerParams(vmem_limit_bytes=24 * MB),
        cost_estimate=pl.CostEstimate(
            flops=5_000_000_000, bytes_accessed=2_000_000, transcendentals=0
        ),
        name="score_last" if last else "score_first",
    )(*operands)


def slots_kernel(t_ref, p_ref, got, owner, out):
    t = t_ref[0]
    first = (p_ref[0] * 8 + t) * ROWS
    best = got[0, 0:8, :]
    for i in range(1, 8):
        best = jnp.maximum(best, got[i, 0:8, :])
    sub = lax.broadcasted_iota(jnp.int32, (8, ROWS), 0)
    scale = jnp.zeros((8, ROWS), F32)
    for i in range(8):
        scale = jnp.where(sub == i, got[i, 8:16, :], scale)
    value = best * scale
    square = jnp.sum(value * value)
    mine = jnp.sum(jnp.where(sub == t, value, 0.0), axis=0, keepdims=True)

    across = jnp.broadcast_to(owner[...].astype(F32), (ROWS, ROWS))
    column = across.T
    row = lax.broadcasted_iota(jnp.int32, (ROWS, ROWS), 0)
    lane = lax.broadcasted_iota(jnp.int32, (ROWS, ROWS), 1)
    earlier = jnp.where((column == across) & (row < lane), 1.0, 0.0)
    rank = jnp.sum(earlier, axis=0, keepdims=True)
    number = (first + 1 + lax.broadcasted_iota(jnp.int32, (1, ROWS), 1)).astype(F32)
    owned = jnp.where(across[0:32] == row[0:32].astype(F32), 1.0, 0.0)
    slot = row.astype(F32)
    filled = jnp.where(slot == rank, mine, 0.0) + jnp.where(slot == rank + CAP, number, 0.0)
    placed = dot_nt(owned, jnp.where(row < 2 * CAP, filled, 0.0), HIGHEST)
    out[...] = jnp.where(lane[0:32] == 2 * CAP, square, placed)


def slots(t, p, got, owner):
    vmem = pl.BlockSpec(memory_space=pltpu.VMEM)
    smem = pl.BlockSpec(memory_space=pltpu.SMEM)
    return pl.pallas_call(
        slots_kernel,
        in_specs=[smem, smem, vmem, vmem],
        out_specs=vmem,
        out_shape=jax.ShapeDtypeStruct((32, ROWS), F32),
        compiler_params=pltpu.CompilerParams(vmem_limit_bytes=4 * MB),
        name="slots",
    )(t[None], p[None], got, owner)


def finish_kernel(tokens, got, weight, token):
    square = jnp.sum(got[:, 2 * CAP : 2 * CAP + 1])
    norm = lax.rsqrt(jnp.full((CAP, 32), square / tokens + 1e-06, F32))
    turned = jnp.concatenate([got[...], jnp.zeros((ROWS - 32, ROWS), F32)], axis=0).T
    weight[...] = turned[0:CAP, 0:32] * norm
    token[...] = turned[CAP : 2 * CAP, 0:32].astype(jnp.int32) - 1


def finish(got, tokens):
    return pl.pallas_call(
        functools.partial(finish_kernel, tokens),
        out_shape=[
            jax.ShapeDtypeStruct((CAP, 32), F32),
            jax.ShapeDtypeStruct((CAP, 32), jnp.int32),
        ],
        compiler_params=pltpu.CompilerParams(vmem_limit_bytes=4 * MB),
        name="finish",
    )(got)


def shift(x, axis, n, k):
    return lax.ppermute(x, axis, [(i, (i + k) % n) for i in range(n)])


def shards(ph, pg, th, tg, fin, fout, example, owner):
    n_tgt = lax.axis_size("tgt")
    n_pool = lax.axis_size("pool")
    t = lax.axis_index("tgt")
    p = lax.axis_index("pool")
    ids = jnp.zeros((16, KH), BF16)
    wide = example.astype(BF16)
    ids = ids.at[0:1, :].set(wide[:, 0:KH])
    ids = ids.at[1:2, :].set(jnp.concatenate([wide[:, KH:TOK]] * 2, axis=1))

    shared = (ph, pg, th, tg, fin, fout.T)
    after = lax.optimization_barrier
    whole = lambda which, slot=0: ((which, slot * MSG, 0, MSG),)
    halves = ((2, 0, 0, MSG // 2), (3, 0, MSG // 2, MSG))
    up, down, opposite_up, opposite_down = project(
        LIMITS[0],
        t,
        (1, 7, 3, 5, 4),
        (whole(0), whole(1), whole(0, 1), whole(1, 1), halves),
        (BF16,) * 4,
        *shared,
    )
    from_low = shift(up, "tgt", n_tgt, 1)
    from_high = shift(down, "tgt", n_tgt, n_tgt - 1)
    half_low = shift(opposite_up, "tgt", n_tgt, 2)
    half_high = shift(opposite_down, "tgt", n_tgt, n_tgt - 2)
    t_next, up = after((t, up))
    two_up, two_down = project(
        LIMITS[1], t_next, (2, 6), (whole(0), whole(1)), (F32, F32), *shared
    )
    two_up, two_down = merge(from_low, from_high, half_low, half_high, two_up, two_down)
    t_next, two_up = after((t, two_up))
    from_low2 = shift(two_up, "tgt", n_tgt, 2)
    from_high2 = shift(two_down, "tgt", n_tgt, n_tgt - 2)
    (own,) = project(LIMITS[2], t_next, (0,), (whole(0),), (F32,), *shared)
    parts = [from_low, from_high, from_low2, from_high2]
    tmsg, pmsg, scale = prepare(own, parts, ids, n_pool // 2)

    same_core = [[2 * i + c for i in range(n_pool // 2)] for c in range(2)]
    near = lax.all_to_all(
        tmsg, "pool", split_axis=0, concat_axis=0, tiled=True, axis_index_groups=same_core
    )
    pools = [pmsg] + [shift(pmsg, "tgt", n_tgt, k) for k in POOL_ORDER]
    near, *pools = after((near, *pools))
    far = lax.ppermute(near, "pool", [(i, i ^ 1) for i in range(n_pool)])
    pin, pout, partial = score(False, *pools, near)
    best = score(True, t[None], pin, pout, partial, far, scale)
    got = lax.all_to_all(best, "tgt", split_axis=0, concat_axis=0, tiled=True)
    sent = slots(t, p, got, owner.T)
    arrived = lax.all_to_all(sent, "pool", split_axis=0, concat_axis=0, tiled=True)
    weight, token = finish(arrived, float(n_pool * n_tgt * ROWS))
    return (weight.T[None, None], token.T[None, None])


def solution(mesh):
    rows = P("pool", "tgt")
    both = P(("pool", "tgt"), None)
    placed = (rows, rows, rows, rows, P("tgt", None), P("tgt", None), both, both)
    return jax.shard_map(
        shards,
        mesh=mesh,
        in_specs=placed,
        out_specs=(P("pool", "tgt", None, None), P("pool", "tgt", None, None)),
        check_vma=False,
    )
```

```python
import functools

import jax
import jax.numpy as jnp
from jax import lax
from jax.experimental import pallas as pl
from jax.experimental.pallas import tpu as pltpu
from jax.sharding import PartitionSpec as P

KH = 128
KG = 64
ROWS = 128
TOK = 192
EX = 16
CAP = 8
GROUP = 8
F32 = jnp.float32
BF16 = jnp.bfloat16
HIGHEST = lax.Precision.HIGHEST
MSG = ROWS + TOK + (ROWS + TOK) // 2
TMSG = TOK + TOK // 2 + 16
PMSG = ROWS + ROWS // 2
MB = 1024 * 1024
LIMITS = (60, 53)
POOL_ORDER = (7, 1, 6, 2, 4, 5, 3)


def dot_nt(a, b, precision=None):
    return lax.dot_general(
        a, b, (((1,), (1,)), ((), ())), preferred_element_type=F32, precision=precision
    )


def lane_mask(shape, low):
    lane = lax.broadcasted_iota(jnp.int32, shape, 1)
    return (lane < KG) if low else (lane >= KG)


def project_kernel(steps, kinds, t_ref, ph, pg, th, tg, fin, fout, *rest):
    outs, (rows_in, rows_out, fin_v, fout_v, sems) = rest[:-5], rest[-5:]
    t = t_ref[0]
    weights = [
        pltpu.make_async_copy(fout, fout_v, sems.at[0, 0]),
        pltpu.make_async_copy(fin, fin_v, sems.at[0, 1]),
    ]
    for copy in weights:
        copy.start()
    moves = []
    both = ROWS + TOK
    for i, k in enumerate(steps):
        who = lax.rem(t + k, 8)
        pool = pl.ds(pl.multiple_of(who * ROWS, ROWS), ROWS)
        tgt = pl.ds(pl.multiple_of(who * TOK, TOK), TOK)
        at_pool = pl.ds(i * both, ROWS)
        at_tgt = pl.ds(i * both + ROWS, TOK)
        here = [
            pltpu.make_async_copy(pg.at[pool, :], rows_out.at[at_pool, :], sems.at[i + 1, 0]),
            pltpu.make_async_copy(tg.at[tgt, :], rows_out.at[at_tgt, :], sems.at[i + 1, 1]),
            pltpu.make_async_copy(ph.at[pool, :], rows_in.at[at_pool, :], sems.at[i + 1, 2]),
            pltpu.make_async_copy(th.at[tgt, :], rows_in.at[at_tgt, :], sems.at[i + 1, 3]),
        ]
        for copy in here:
            copy.start()
        moves.append(here)
    for copy in weights:
        copy.wait()
    together = len(steps)
    for first in range(0, len(steps), together):
        count = min(together, len(steps) - first)
        for i in range(first, first + count):
            for copy in moves[i]:
                copy.wait()
        rows = slice(first * both, (first + count) * both)
        sums_out = dot_nt(rows_out[rows, :], fout_v[...])
        sums_in = jnp.dot(rows_in[rows, :], fin_v[...], preferred_element_type=F32)
        for i in range(first, first + count):
            lead = (i - first) * both
            message = [sums_in[lead : lead + both]]
            for size in (ROWS, TOK):
                half = size // 2
                message.append(
                    jnp.concatenate(
                        [sums_out[lead : lead + half], sums_out[lead + half : lead + size]], axis=1
                    )
                )
                lead = lead + size
            message = jnp.concatenate(message, axis=0)
            for which, at, start, stop in kinds[i]:
                out = outs[which]
                out[at : at + stop - start, :] = message[start:stop].astype(out.dtype)


def project(limit, t, steps, kinds, dtypes, ph, pg, th, tg, fin, fout):
    n = len(steps)
    pieces = [piece for kind in kinds for piece in kind]
    sizes = [sum(p[3] - p[2] for p in pieces if p[0] == j) for j in range(len(dtypes))]
    hbm = pl.BlockSpec(memory_space=pltpu.HBM)
    vmem = pl.BlockSpec(memory_space=pltpu.VMEM)
    return pl.pallas_call(
        functools.partial(project_kernel, steps, kinds),
        in_specs=[pl.BlockSpec(memory_space=pltpu.SMEM)] + [hbm] * 6,
        out_specs=[vmem for _ in dtypes],
        out_shape=[jax.ShapeDtypeStruct((c, KH), d) for c, d in zip(sizes, dtypes)],
        scratch_shapes=[
            pltpu.VMEM((n * (ROWS + TOK), ph.shape[1]), BF16),
            pltpu.VMEM((n * (ROWS + TOK), pg.shape[1]), BF16),
            pltpu.VMEM(fin.shape, BF16),
            pltpu.VMEM(fout.shape, BF16),
            pltpu.SemaphoreType.DMA((n + 1, 4)),
        ],
        compiler_params=pltpu.CompilerParams(vmem_limit_bytes=limit * MB),
        cost_estimate=pl.CostEstimate(
            flops=n * 170_000_000, bytes_accessed=n * 1_600_000, transcendentals=0
        ),
        name="project",
    )(t[None], ph, pg, th, tg, fin, fout)


def merge_kernel(from_low, from_high, half_low, half_high, mine_up, mine_down, up, down):
    half = MSG // 2
    total = mine_up[...] + from_low[MSG : 2 * MSG, :].astype(F32)
    up[0:half, :] = (total[0:half] + half_low[...].astype(F32)).astype(BF16)
    up[half:MSG, :] = total[half:MSG].astype(BF16)
    total = mine_down[...] + from_high[MSG : 2 * MSG, :].astype(F32)
    down[0:half, :] = total[0:half].astype(BF16)
    down[half:MSG, :] = (total[half:MSG] + half_high[...].astype(F32)).astype(BF16)


def merge(*operands):
    return pl.pallas_call(
        merge_kernel,
        out_shape=[jax.ShapeDtypeStruct((MSG, KH), BF16)] * 2,
        compiler_params=pltpu.CompilerParams(vmem_limit_bytes=8 * MB),
        cost_estimate=pl.CostEstimate(flops=200_000, bytes_accessed=1_500_000, transcendentals=0),
        name="merge",
    )(*operands)


def prepare_kernel(own, *rest):
    parts, (ids_ref, tmsg, pmsg, scale_ref, message, sems) = rest[:-6], rest[-6:]
    total = own[...]
    for part in parts:
        total = total + part[0:MSG, :].astype(F32)
    pool_in = total[0:ROWS]
    tgt_in = total[ROWS : ROWS + TOK]
    pool_out = total[ROWS + TOK : ROWS + TOK + ROWS // 2]
    tgt_out = total[ROWS + TOK + ROWS // 2 : MSG]

    ids = ids_ref[...].astype(F32)
    first = ids[0:1, :]
    second = jnp.where(lane_mask((1, KH), True), ids[1:2, :], -1.0)
    column = jnp.concatenate(
        [jnp.broadcast_to(first, (KH, KH)).T, jnp.broadcast_to(second, (KH, KH)).T], axis=0
    )
    same = jnp.concatenate([column == first, column == second], axis=1)
    pad = jnp.zeros((2 * KH - TOK, KH), F32)
    wide_in = jnp.concatenate([tgt_in, pad], axis=0)
    low = lane_mask(tgt_out.shape, True)
    zero = jnp.zeros_like(tgt_out)
    wide_out = jnp.concatenate(
        [
            jnp.where(low, tgt_out, zero),
            jnp.where(low, pltpu.roll(tgt_out, KG, 1), zero),
            pad,
        ],
        axis=0,
    )
    message[TOK : TOK + TOK // 2, :] = tgt_out.astype(BF16)
    message[TOK + TOK // 2 : TMSG, :] = ids_ref[...]
    copies = []
    for i in range(tmsg.shape[0]):
        for j, rows in enumerate((slice(TOK, TMSG), slice(0, TOK))):
            here, there = message.at[rows, :], tmsg.at[i, rows, :]
            copies.append(pltpu.make_async_copy(here, there, sems.at[i, j]))
    for copy in copies[0::2]:
        copy.start()
    gram = dot_nt(wide_in, wide_in, HIGHEST) * dot_nt(wide_out, wide_out, HIGHEST)
    spread = jnp.sum(jnp.where(same, gram, 0.0), axis=0, keepdims=True)
    token_sq = jnp.sum(jnp.where(same, spread, 0.0), axis=1, keepdims=True)
    message[0:TOK, :] = (tgt_in * lax.rsqrt(token_sq[0:TOK] + 1e-06)).astype(BF16)
    for copy in copies[1::2]:
        copy.start()

    pmsg[0:ROWS, :] = pool_in.astype(BF16)
    pmsg[ROWS:PMSG, :] = pool_out.astype(BF16)
    low = lane_mask(pool_out.shape, True)
    zero = jnp.zeros_like(pool_out)
    out_rows = jnp.concatenate(
        [jnp.where(low, pool_out, zero), jnp.where(low, zero, pool_out)], axis=0
    )
    in_sq = jnp.sum((pool_in * pool_in).T, axis=0, keepdims=True)
    out_sq = jnp.sum((out_rows * out_rows).T, axis=0, keepdims=True)
    scale_ref[...] = jnp.broadcast_to(lax.rsqrt(in_sq * out_sq + 1e-06), scale_ref.shape)
    for copy in copies:
        copy.wait()


def prepare(own, parts, ids, copies):
    vmem = pl.BlockSpec(memory_space=pltpu.VMEM)
    return pl.pallas_call(
        prepare_kernel,
        out_specs=[pl.BlockSpec(memory_space=pl.ANY), vmem, vmem],
        out_shape=[
            jax.ShapeDtypeStruct((copies, TMSG, KH), BF16),
            jax.ShapeDtypeStruct((PMSG, KH), BF16),
            jax.ShapeDtypeStruct((8, ROWS), F32),
        ],
        scratch_shapes=[pltpu.VMEM((TMSG, KH), BF16), pltpu.SemaphoreType.DMA((copies, 2))],
        compiler_params=pltpu.CompilerParams(vmem_limit_bytes=24 * MB),
        cost_estimate=pl.CostEstimate(flops=200_000_000, bytes_accessed=3_000_000, transcendentals=0),
        name="prepare",
    )(own, *parts, ids)


def score_kernel(last, *refs):
    if last:
        t_ref, pin, pout, prev, tmsg, scale, out, t_in, t_out, hot, best, rows = refs
    else:
        pools, (tmsg, pin, pout, best, t_in, t_out, hot) = refs[:8], refs[8:]
        half = ROWS // 2
        low = lane_mask((half, KH), True)
        for k, pool in zip((0,) + POOL_ORDER, pools):
            at = k * ROWS
            pin[at : at + ROWS, :] = pool[0:ROWS, :]
            packed = pool[ROWS:PMSG, :].astype(F32)
            turned = pltpu.roll(packed, KG, 1)
            pout[at : at + half, :] = jnp.where(low, packed, turned).astype(BF16)
            pout[at + half : at + ROWS, :] = jnp.where(low, turned, packed).astype(BF16)

    lane = lax.broadcasted_iota(jnp.int32, (1, KH), 1)
    keep_low = (lane < KG).astype(F32).astype(BF16)
    keep_high = (lane >= KG).astype(F32).astype(BF16)
    width = GROUP * TOK
    tile = 512
    example = lax.broadcasted_iota(jnp.int32, (GROUP * EX, KH), 0).astype(F32)

    groups = tmsg.shape[0] // GROUP
    for g in range(groups):
        for pair in range(GROUP // 2):
            b0 = g * GROUP + 2 * pair
            b1 = b0 + 1
            at = b0 * TOK
            t_in[at : at + TOK, :] = tmsg[b0, 0:TOK, :]
            t_in[at + TOK : at + TOK + 64, :] = tmsg[b1, 128:TOK, :]
            t_in[at + TOK + 64 : at + 2 * TOK, :] = tmsg[b1, 0:128, :]
            o0 = tmsg[b0, TOK : TOK + 96, :]
            o1 = tmsg[b1, TOK : TOK + 96, :]
            t_out[at : at + 96, :] = o0 * keep_low
            t_out[at + 96 : at + TOK, :] = o0 * keep_high
            t_out[at + TOK : at + TOK + 64, :] = o1[32:96] * keep_high
            t_out[at + TOK + 64 : at + TOK + 160, :] = o1 * keep_low
            t_out[at + TOK + 160 : at + 2 * TOK, :] = o1[0:32] * keep_high
            i0 = tmsg[b0, TOK + 96 : TMSG, :].astype(F32) + float(2 * pair * EX)
            i1 = tmsg[b1, TOK + 96 : TMSG, :].astype(F32) + float((2 * pair + 1) * EX)
            mixed = jnp.where(lane < KG, i0[1:2, :], i1[1:2, :])
            hot[:, at : at + 128] = (example == i0[0:1, :]).astype(F32).astype(BF16)
            hot[:, at + 128 : at + 256] = (example == mixed).astype(F32).astype(BF16)
            hot[:, at + 256 : at + 384] = (example == i1[0:1, :]).astype(F32).astype(BF16)
    for g in range(groups):
        total = None
        for i in range(width // tile):
            cols = slice(g * width + i * tile, g * width + (i + 1) * tile)
            joined = dot_nt(pin[...], t_in[cols, :]) * dot_nt(pout[...], t_out[cols, :])
            part = dot_nt(joined.astype(BF16), hot[:, cols])
            total = part if total is None else total + part
        if last or g:
            so_far = best if g else prev
            best[...] = jnp.maximum(so_far[...], total)
        else:
            best[...] = total
    if last:
        t = t_ref[0]
        for k in range(8):
            row = jnp.max(best[k * ROWS : (k + 1) * ROWS, :].T, axis=0, keepdims=True)
            rows[pl.ds(lax.rem(t + 8 - k, 8), 1), :] = row
        for i in range(out.shape[0]):
            out[i, 0:8, :] = rows[...]
            out[i, 8:16, :] = scale[...]


def score(last, *operands):
    tokens = operands[-2 if last else -1].shape[0] * TOK
    vmem = pl.BlockSpec(memory_space=pltpu.VMEM)
    smem = pl.BlockSpec(memory_space=pltpu.SMEM)
    unpacked = jax.ShapeDtypeStruct((8 * ROWS, KH), BF16)
    maxima = jax.ShapeDtypeStruct((8 * ROWS, GROUP * EX), F32)
    message = jax.ShapeDtypeStruct((8, 16, ROWS), F32)
    scratch = [
        pltpu.VMEM((tokens, KH), BF16),
        pltpu.VMEM((tokens, KH), BF16),
        pltpu.VMEM((GROUP * EX, tokens), BF16),
    ]
    if last:
        scratch += [pltpu.VMEM(maxima.shape, F32), pltpu.VMEM((8, ROWS), F32)]
    return pl.pallas_call(
        functools.partial(score_kernel, last),
        in_specs=[smem] * last + [vmem] * (len(operands) - last),
        out_specs=vmem if last else [vmem] * 3,
        out_shape=message if last else [unpacked, unpacked, maxima],
        scratch_shapes=scratch,
        compiler_params=pltpu.CompilerParams(vmem_limit_bytes=24 * MB),
        cost_estimate=pl.CostEstimate(
            flops=5_000_000_000, bytes_accessed=2_000_000, transcendentals=0
        ),
        name="score_last" if last else "score_first",
    )(*operands)


def slots_kernel(t_ref, p_ref, got, owner, out):
    t = t_ref[0]
    first = (p_ref[0] * 8 + t) * ROWS
    best = got[0, 0:8, :]
    for i in range(1, 8):
        best = jnp.maximum(best, got[i, 0:8, :])
    sub = lax.broadcasted_iota(jnp.int32, (8, ROWS), 0)
    scale = jnp.zeros((8, ROWS), F32)
    for i in range(8):
        scale = jnp.where(sub == i, got[i, 8:16, :], scale)
    value = best * scale
    square = jnp.sum(value * value)
    mine = jnp.sum(jnp.where(sub == t, value, 0.0), axis=0, keepdims=True)

    across = jnp.broadcast_to(owner[...].astype(F32), (ROWS, ROWS))
    column = across.T
    row = lax.broadcasted_iota(jnp.int32, (ROWS, ROWS), 0)
    lane = lax.broadcasted_iota(jnp.int32, (ROWS, ROWS), 1)
    earlier = jnp.where((column == across) & (row < lane), 1.0, 0.0)
    rank = jnp.sum(earlier, axis=0, keepdims=True)
    number = (first + 1 + lax.broadcasted_iota(jnp.int32, (1, ROWS), 1)).astype(F32)
    owned = jnp.where(across[0:32] == row[0:32].astype(F32), 1.0, 0.0)
    slot = row.astype(F32)
    filled = jnp.where(slot == rank, mine, 0.0) + jnp.where(slot == rank + CAP, number, 0.0)
    placed = dot_nt(owned, jnp.where(row < 2 * CAP, filled, 0.0), HIGHEST)
    out[...] = jnp.where(lane[0:32] == 2 * CAP, square, placed)


def slots(t, p, got, owner):
    vmem = pl.BlockSpec(memory_space=pltpu.VMEM)
    smem = pl.BlockSpec(memory_space=pltpu.SMEM)
    return pl.pallas_call(
        slots_kernel,
        in_specs=[smem, smem, vmem, vmem],
        out_specs=vmem,
        out_shape=jax.ShapeDtypeStruct((32, ROWS), F32),
        compiler_params=pltpu.CompilerParams(vmem_limit_bytes=4 * MB),
        name="slots",
    )(t[None], p[None], got, owner)


def finish_kernel(tokens, got, weight, token):
    square = jnp.sum(got[:, 2 * CAP : 2 * CAP + 1])
    norm = lax.rsqrt(jnp.full((CAP, 32), square / tokens + 1e-06, F32))
    turned = jnp.concatenate([got[...], jnp.zeros((ROWS - 32, ROWS), F32)], axis=0).T
    weight[...] = turned[0:CAP, 0:32] * norm
    token[...] = turned[CAP : 2 * CAP, 0:32].astype(jnp.int32) - 1


def finish(got, tokens):
    return pl.pallas_call(
        functools.partial(finish_kernel, tokens),
        out_shape=[
            jax.ShapeDtypeStruct((CAP, 32), F32),
            jax.ShapeDtypeStruct((CAP, 32), jnp.int32),
        ],
        compiler_params=pltpu.CompilerParams(vmem_limit_bytes=4 * MB),
        name="finish",
    )(got)


def shift(x, axis, n, k):
    return lax.ppermute(x, axis, [(i, (i + k) % n) for i in range(n)])


def shards(ph, pg, th, tg, fin, fout, example, owner):
    n_tgt = lax.axis_size("tgt")
    n_pool = lax.axis_size("pool")
    t = lax.axis_index("tgt")
    p = lax.axis_index("pool")
    ids = jnp.zeros((16, KH), BF16)
    wide = example.astype(BF16)
    ids = ids.at[0:1, :].set(wide[:, 0:KH])
    ids = ids.at[1:2, :].set(jnp.concatenate([wide[:, KH:TOK]] * 2, axis=1))

    shared = (ph, pg, th, tg, fin, fout.T)
    after = lax.optimization_barrier
    whole = lambda which, slot=0: ((which, slot * MSG, 0, MSG),)
    halves = ((2, 0, 0, MSG // 2), (3, 0, MSG // 2, MSG))
    up, down, opposite_up, opposite_down = project(
        LIMITS[0],
        t,
        (1, 7, 3, 5, 4),
        (whole(0), whole(1), whole(0, 1), whole(1, 1), halves),
        (BF16,) * 4,
        *shared,
    )
    from_low = shift(up, "tgt", n_tgt, 1)
    from_high = shift(down, "tgt", n_tgt, n_tgt - 1)
    half_low = shift(opposite_up, "tgt", n_tgt, 2)
    half_high = shift(opposite_down, "tgt", n_tgt, n_tgt - 2)
    t_next, up = after((t, up))
    two_up, two_down, own = project(
        LIMITS[1], t_next, (2, 6, 0), (whole(0), whole(1), whole(2)), (F32,) * 3, *shared
    )
    two_up, two_down = merge(from_low, from_high, half_low, half_high, two_up, two_down)
    from_low2 = shift(two_up, "tgt", n_tgt, 2)
    from_high2 = shift(two_down, "tgt", n_tgt, n_tgt - 2)
    parts = [from_low, from_high, from_low2, from_high2]
    tmsg, pmsg, scale = prepare(own, parts, ids, n_pool // 2)

    same_core = [[2 * i + c for i in range(n_pool // 2)] for c in range(2)]
    near = lax.all_to_all(
        tmsg, "pool", split_axis=0, concat_axis=0, tiled=True, axis_index_groups=same_core
    )
    pools = [pmsg] + [shift(pmsg, "tgt", n_tgt, k) for k in POOL_ORDER]
    near, *pools = after((near, *pools))
    far = lax.ppermute(near, "pool", [(i, i ^ 1) for i in range(n_pool)])
    pin, pout, partial = score(False, *pools, near)
    best = score(True, t[None], pin, pout, partial, far, scale)
    got = lax.all_to_all(best, "tgt", split_axis=0, concat_axis=0, tiled=True)
    sent = slots(t, p, got, owner.T)
    arrived = lax.all_to_all(sent, "pool", split_axis=0, concat_axis=0, tiled=True)
    weight, token = finish(arrived, float(n_pool * n_tgt * ROWS))
    return (weight.T[None, None], token.T[None, None])


def solution(mesh):
    rows = P("pool", "tgt")
    both = P(("pool", "tgt"), None)
    placed = (rows, rows, rows, rows, P("tgt", None), P("tgt", None), both, both)
    return jax.shard_map(
        shards,
        mesh=mesh,
        in_specs=placed,
        out_specs=(P("pool", "tgt", None, None), P("pool", "tgt", None, None)),
        check_vma=False,
    )
```
